32 devices in a mesh: clip: 4 (over z), seq: 8 (over y, x, core).
Axes of the slice: x: 2, y: 2, z: 4, core: 2. Of those that a mesh axis runs over, the one named last changes fastest.
Arguments:
- query_in: bfloat16 [4096, 4096], P(('clip', 'seq')), parts along dimension 0, may hold values from -12 to 12
- key_in: bfloat16 [4096, 4096], P(('clip', 'seq')), parts along dimension 0, may hold values from -12 to 12
- value_in: bfloat16 [4096, 4096], P(('clip', 'seq')), parts along dimension 0, may hold values from -6 to 6
- grad_out: bfloat16 [4096, 4096], P(('clip', 'seq')), parts along dimension 0, may hold values from -6 to 6
- positions: int32 [3, 4096], P(None, 'clip'), parts along dimension 1, may hold values from 0 to 15, as said below
- block_flags: int32 [32, 8], P('clip'), parts along dimension 0, may hold values from 0 to 1, as said below
- band_ids: int32 [32, 8], P('clip'), parts along dimension 0, may hold values from 0 to 3, as said below
Outputs:
- attn_out: bfloat16 [4096, 4096], P(('clip', 'seq')), parts along dimension 0
- grad_query: bfloat16 [4096, 4096], P(('clip', 'seq')), parts along dimension 0
- grad_key: bfloat16 [4096, 4096], P(('clip', 'seq')), parts along dimension 0
- grad_value: bfloat16 [4096, 4096], P(('clip', 'seq')), parts along dimension 0
The draws below stay inside these ranges and needn't reach their ends.
There are 4 independent parts, one for each index of `clip`. The reference program is written for one: setup_inputs(seed, part) draws one part's arguments, and reference() takes and returns one part's arrays. A program takes and returns all parts, laid end to end along the dimension named above; each array names one. Nothing has to cross between parts.
Inputs may be any that keep to these rules, and one draw needn't show every extreme that they name: positions[0] is the latent frame of a token: tokens come in frames of 256, frame numbers rise strictly from frame to frame and may skip, and the last frame's number is 7; positions[1] and positions[2] are row and column in a square crop, row-major. `block_flags`: diagonal block pairs are always 1. `band_ids`: diagonal block pairs are 0.
All inputs are finite; a program needn't handle non-finite values.
Results may differ from the reference program's by a relative error of at most 0.015.
Values may be sent and summed in bfloat16 or wider, within the bound.
No kernel may reach another device: no remote copies, remote signals or barrier semaphores. Data moves between devices by JAX's collectives and lax.ppermute only.
A program may use at most 128 MiB of HBM per device.

```python
import math
import jax
import jax.numpy as jnp
from jax import lax

H = 32
DH = 128
BLK = 128
FRAME_TOK = 256
TOKENS = 1024


def queries_and_keys(key):
    shape_all = (TOKENS, H * DH)
    query_all = jax.random.truncated_normal(jax.random.fold_in(key, 1), -6.0, 6.0, shape_all, jnp.float32)
    key_all = jax.random.truncated_normal(jax.random.fold_in(key, 2), -6.0, 6.0, shape_all, jnp.float32)
    return (query_all, key_all)


def draw_query_in(key, part):
    return queries_and_keys(key)[0].astype(jnp.bfloat16)


def draw_key_in(key, part):
    return queries_and_keys(key)[1].astype(jnp.bfloat16)


def draw_positions(key, part):
    frames_all = TOKENS // FRAME_TOK
    order = jax.random.permutation(jax.random.fold_in(key, 21), 2 * frames_all - 1)[:frames_all - 1]
    earlier_frames = jnp.sort(order).astype(jnp.int32)
    last_frame = jnp.full((1,), 2 * frames_all - 1, jnp.int32)
    chosen_frames = jnp.concatenate([earlier_frames, last_frame], 0)
    row_ids = jnp.arange(TOKENS, dtype=jnp.int32)
    side_len = int(math.isqrt(FRAME_TOK))
    frame_num = chosen_frames[row_ids // FRAME_TOK]
    row_num = row_ids % FRAME_TOK // side_len
    column_num = row_ids % side_len
    return jnp.stack([frame_num, row_num, column_num], 0).astype(jnp.int32)


def mask_pair(key):
    blocks_all = TOKENS // BLK
    per_frame = FRAME_TOK // BLK
    block_ids = jnp.arange(blocks_all, dtype=jnp.int32)
    frame_gap = jnp.abs(block_ids[:, None] // per_frame - block_ids[None, :] // per_frame)
    level = (frame_gap >= 1).astype(jnp.int32) + (frame_gap >= 2).astype(jnp.int32) + (frame_gap >= 4).astype(jnp.int32)
    extra = jax.random.randint(jax.random.fold_in(key, 31), (blocks_all, blocks_all), 0, 2)
    diagonal = block_ids[:, None] == block_ids[None, :]
    band_all = jnp.where(diagonal, 0, jnp.minimum(level + extra, 3)).astype(jnp.int32)
    rolled = jax.random.randint(jax.random.fold_in(key, 32), (blocks_all, blocks_all), 0, 8)
    flag_all = jnp.where(diagonal, 1, (rolled < jnp.right_shift(jnp.int32(8), band_all)).astype(jnp.int32)).astype(jnp.int32)
    return (flag_all, band_all)


def draw_block_flags(key, part):
    return mask_pair(key)[0]


def draw_band_ids(key, part):
    return mask_pair(key)[1]


def level_of(stream_key, extent, shards, smallest, top_value):
    loudness, own = 1.0, jax.random.fold_in(stream_key, 6)
    for dim, parts in shards:
        heights = jnp.exp(jax.random.uniform(jax.random.fold_in(own, dim), (parts,), jnp.float32, smallest / len(shards), top_value / len(shards)))
        loudness = loudness * jnp.repeat(heights, extent[dim] // parts).reshape([-1 if axis == dim else 1 for axis in range(len(extent))])
    return loudness


def bell_draw(key, shape, spread, limit, pieces=(), kind=jnp.bfloat16):
    result = spread * jax.random.normal(key, shape, jnp.float32)
    if pieces:
        result = result * level_of(key, shape, pieces, -0.22, 0.18)
    return jnp.clip(result, -limit, limit).astype(kind)


def setup_inputs(seed: int = 0, part: int = 0) -> dict:
    seeds = jax.random.split(jax.random.key(seed), 8)
    part_splits = jax.random.split(jax.random.fold_in(seeds[7], part), 8)
    query_in = draw_query_in(jax.random.fold_in(jax.random.fold_in(seeds[7], part), 71), part)
    key_in = draw_key_in(jax.random.fold_in(jax.random.fold_in(seeds[7], part), 71), part)
    value_in = bell_draw(part_splits[2], (TOKENS, H * DH), 1.0, 6.0, ((0, 8),))
    grad_out = bell_draw(part_splits[3], (TOKENS, H * DH), 1.0, 6.0, ((0, 8),))
    positions = draw_positions(jax.random.fold_in(jax.random.fold_in(seeds[7], part), 71), part)
    block_flags = draw_block_flags(jax.random.fold_in(jax.random.fold_in(seeds[7], part), 71), part)
    band_ids = draw_band_ids(jax.random.fold_in(jax.random.fold_in(seeds[7], part), 71), part)
    return dict(query_in=query_in, key_in=key_in, value_in=value_in, grad_out=grad_out, positions=positions, block_flags=block_flags, band_ids=band_ids)


ntk_factor = 2.0

def rope_tables(positions):
    third_part = 2 * (DH // 6)
    part_dims = (DH - 2 * third_part, third_part, third_part)
    angle_parts = []
    for axis_num, piece_dim in enumerate(part_dims):
        base_freq = 10000.0 * ntk_factor ** (piece_dim / (piece_dim - 2.0))
        pair_index = jnp.arange(piece_dim // 2, dtype=jnp.float32)
        inverse = jnp.exp(pair_index * (-2.0 * math.log(base_freq) / piece_dim))
        angle_parts.append(positions[axis_num].astype(jnp.float32)[:, None] * inverse[None, :])
    angle_all = jnp.concatenate(angle_parts, 1)
    return (jnp.cos(angle_all), jnp.sin(angle_all))

def rotate(values, cosine_table, sine_table):
    shape_all = values.shape
    paired = values.reshape(shape_all[:-1] + (shape_all[-1] // 2, 2))
    even_part = paired[..., 0]
    odd_part = paired[..., 1]
    cos_wide = cosine_table[:, None, :]
    sin_wide = sine_table[:, None, :]
    turned = jnp.stack([even_part * cos_wide - odd_part * sin_wide, odd_part * cos_wide + even_part * sin_wide], -1)
    return turned.reshape(shape_all)

def block_mask(block_flags, band_ids, first_row, row_count):
    blocks_all = block_flags.shape[1]
    rows_blocks = row_count // BLK
    start_block = first_row // BLK
    flag_rows = lax.dynamic_slice_in_dim(block_flags, start_block, rows_blocks, 0)
    band_rows = lax.dynamic_slice_in_dim(band_ids, start_block, rows_blocks, 0)
    reach_width = jnp.right_shift(jnp.int32(BLK), band_rows)
    offsets = jnp.arange(BLK, dtype=jnp.int32)
    apart_rows = jnp.abs(offsets[:, None] - offsets[None, :])
    keep_mask = (flag_rows[:, None, :, None] == 1) & (apart_rows[None, :, None, :] < reach_width[:, None, :, None])
    return keep_mask.reshape(row_count, blocks_all * BLK)

def reference(query_in, key_in, value_in, grad_out, positions, block_flags, band_ids):
    cosine_table, sine_table = rope_tables(positions)
    allowed = block_mask(block_flags, band_ids, 0, TOKENS)
    score_scale = 1.0 / math.sqrt(DH)

    def split_heads(operand):
        return operand.reshape(TOKENS, H, DH).transpose(1, 0, 2)

    def one_head(operands):
        head_query, head_key, head_value, head_grad = operands
        query_rot = rotate(head_query.astype(jnp.float32)[:, None, :], cosine_table, sine_table)[:, 0, :].astype(jnp.bfloat16)
        key_rot = rotate(head_key.astype(jnp.float32)[:, None, :], cosine_table, sine_table)[:, 0, :].astype(jnp.bfloat16)
        scores = jnp.dot(query_rot, key_rot.T, preferred_element_type=jnp.float32) * score_scale
        scores = jnp.where(allowed, scores, -jnp.inf)
        largest = lax.optimization_barrier(jnp.max(scores, axis=1, keepdims=True))
        weights = jnp.exp(scores - largest)
        probs = weights / lax.optimization_barrier(jnp.sum(weights, axis=1, keepdims=True))
        probs_low = probs.astype(jnp.bfloat16)
        attn_head = jnp.dot(probs_low, head_value, preferred_element_type=jnp.float32).astype(jnp.bfloat16)
        delta_sum = lax.optimization_barrier(jnp.sum(head_grad.astype(jnp.float32) * attn_head.astype(jnp.float32), axis=1))
        grad_probs = jnp.dot(head_grad, head_value.T, preferred_element_type=jnp.float32)
        grad_scores = (probs * (grad_probs - delta_sum[:, None]) * score_scale).astype(jnp.bfloat16)
        grad_value_head = jnp.dot(probs_low.T, head_grad, preferred_element_type=jnp.float32).astype(jnp.bfloat16)
        grad_query_rot = jnp.dot(grad_scores, key_rot, preferred_element_type=jnp.float32)
        grad_key_rot = jnp.dot(grad_scores.T, query_rot, preferred_element_type=jnp.float32)
        grad_query_head = rotate(grad_query_rot[:, None, :], cosine_table, -sine_table)[:, 0, :].astype(jnp.bfloat16)
        grad_key_head = rotate(grad_key_rot[:, None, :], cosine_table, -sine_table)[:, 0, :].astype(jnp.bfloat16)
        return (attn_head, grad_query_head, grad_key_head, grad_value_head)
    results = lax.map(one_head, (split_heads(query_in), split_heads(key_in), split_heads(value_in), split_heads(grad_out)))

    def join_heads(operand):
        return operand.transpose(1, 0, 2).reshape(TOKENS, H * DH)
    return (join_heads(results[0]), join_heads(results[1]), join_heads(results[2]), join_heads(results[3]))
```

```python
import functools
import math

import jax
import jax.numpy as jnp
from jax import lax
from jax.experimental import pallas as pl
from jax.experimental.pallas import tpu as pltpu
from jax.sharding import PartitionSpec as P

H = 32
DH = 128
BLK = 128
NTK = 2.0
CHUNKS = 2

F32 = jnp.float32
BF16 = jnp.bfloat16
NEG_INF = float("-inf")


def rope_tables(positions):
    third = 2 * (DH // 6)
    part_dims = (DH - 2 * third, third, third)
    pieces = []
    for axis_num, dim in enumerate(part_dims):
        base = 10000.0 * NTK ** (dim / (dim - 2.0))
        pair = (jnp.arange(dim, dtype=jnp.int32) // 2).astype(F32)
        inverse = jnp.exp(pair * (-2.0 * math.log(base) / dim))
        pieces.append(positions[axis_num].astype(F32)[:, None] * inverse[None, :])
    angle = jnp.concatenate(pieces, 1)
    sign = jnp.where(jnp.arange(DH, dtype=jnp.int32) % 2 == 0, -1.0, 1.0).astype(F32)
    return jnp.cos(angle), jnp.sin(angle) * sign[None, :]


def pack_kernel(groups, heads, first, count, me_ref, q_ref, k_ref, v_ref, g_ref, *rest):
    outs, sems = rest[:groups], rest[groups]
    me = me_ref[0]
    copies = []
    for d in range(groups):
        start = pl.multiple_of(((me ^ d) * heads + first) * DH, DH)
        for a, ref in enumerate((q_ref, k_ref, v_ref, g_ref)):
            copies.append(
                pltpu.make_async_copy(
                    ref.at[:, pl.ds(start, count * DH)], outs[d].at[a], sems.at[d, a]
                )
            )
    for copy in copies:
        copy.start()
    for copy in copies:
        copy.wait()


def unpack_kernel(groups, heads, first, count, kept, me_ref, *rest):
    pieces = rest[:groups]
    outs = rest[groups + kept : groups + kept + 4]
    sems = rest[groups + kept + 4]
    me = me_ref[0]
    copies = []
    for d in range(groups):
        start = pl.multiple_of(((me ^ d) * heads + first) * DH, DH)
        for a in range(4):
            copies.append(
                pltpu.make_async_copy(
                    pieces[d].at[a], outs[a].at[:, pl.ds(start, count * DH)], sems.at[d, a]
                )
            )
    for copy in copies:
        copy.start()
    for copy in copies:
        copy.wait()


def dot(x, y):
    return jnp.dot(x, y, preferred_element_type=F32)


def dot_t(x, y):
    return lax.dot_general(x, y, (((1,), (1,)), ((), ())), preferred_element_type=F32)


def attention_kernel(groups, rows, count, width, me_ref, flags_ref, bands_ref, cos_ref, sin_ref, *rest):
    ins, outs = rest[:groups], rest[groups : 2 * groups]
    qr, kr, vs, gs, kt, vt, gt, scores, low, ds, dk, dv, os, dqs = rest[2 * groups :]
    total = groups * rows
    per_piece = rows // BLK
    blocks = total // BLK
    scale = 1.0 / math.sqrt(DH)
    score_factor = scale / math.log(2.0)
    me = me_ref[0]

    even = lax.broadcasted_iota(jnp.int32, (rows, DH), 1) % 2 == 0
    apart = jnp.abs(
        lax.broadcasted_iota(jnp.int32, (BLK, BLK), 0) - lax.broadcasted_iota(jnp.int32, (BLK, BLK), 1)
    )

    def turn(x, cos, sin):
        partner = jnp.where(even, pltpu.roll(x, DH - 1, 1), pltpu.roll(x, 1, 1))
        return x * cos + partner * sin

    def table_rows(d):
        return pl.ds(pl.multiple_of((me ^ d) * rows, rows), rows)

    def block_of(b):
        return (me ^ (b // per_piece)) * per_piece + b % per_piece

    def one_head(h, carry):
        cols = pl.ds(pl.multiple_of(h * DH, DH), DH)
        for d in range(groups):
            at = slice(d * rows, (d + 1) * rows)
            cos, sin = cos_ref[table_rows(d), :], sin_ref[table_rows(d), :]
            qr[at, :] = turn(ins[d][0, :, cols].astype(F32), cos, sin).astype(BF16)
            key = turn(ins[d][1, :, cols].astype(F32), cos, sin).astype(BF16)
            kr[at, :] = key
            kt[:, at] = key.T
            value = ins[d][2, :, cols]
            vs[at, :] = value
            vt[:, at] = value.T
            grad = ins[d][3, :, cols]
            gs[at, :] = grad
            gt[:, at] = grad.T
        dk[...] = jnp.zeros_like(dk)
        dv[...] = jnp.zeros_like(dv)

        def one_step(i, carry):
            mine = pl.ds(pl.multiple_of(i * width, width), width)
            query, grad = qr[mine, :], gs[mine, :]
            top = jnp.full((8, width), NEG_INF, F32)
            for j in range(blocks):
                at = slice(j * BLK, (j + 1) * BLK)
                raw = dot_t(kr[at, :], query) * score_factor
                parts = []
                for w in range(width // BLK):
                    row, col = block_of(i * (width // BLK) + w), block_of(j)
                    reach = jnp.where(
                        flags_ref[row, col] == 1, jnp.right_shift(BLK, bands_ref[row, col]), 0
                    )
                    parts.append(jnp.where(apart < reach, raw[:, w * BLK : (w + 1) * BLK], NEG_INF))
                part = jnp.concatenate(parts, 1)
                scores[at, :] = part
                top = jnp.maximum(top, jnp.max(part.reshape(BLK // 8, 8, width), axis=0))
            largest = jnp.max(top, axis=0, keepdims=True)
            norm = jnp.zeros((8, width), F32)
            for j in range(blocks):
                at = slice(j * BLK, (j + 1) * BLK)
                weights = jnp.exp2(scores[at, :] - largest)
                scores[at, :] = weights
                norm = norm + jnp.sum(weights.reshape(BLK // 8, 8, width), axis=0)
            inverse = 1.0 / jnp.sum(norm, axis=0, keepdims=True)
            for j in range(blocks):
                at = slice(j * BLK, (j + 1) * BLK)
                probs = scores[at, :] * inverse
                scores[at, :] = probs
                low[at, :] = probs.astype(BF16)
            out_t = dot(vt[...], low[...]).astype(BF16).astype(F32)
            delta = jnp.sum(out_t * gt[:, mine].astype(F32), axis=0, keepdims=True)
            os[mine, :] = out_t.T.astype(BF16)
            for j in range(blocks):
                at = slice(j * BLK, (j + 1) * BLK)
                grad_probs = dot_t(vs[at, :], grad)
                ds[at, :] = (scores[at, :] * (grad_probs - delta)).astype(BF16)
            dqs[mine, :] = dot(kt[...], ds[...]).T
            dv[...] += dot(low[...], grad)
            dk[...] += dot(ds[...], query)
            return carry

        lax.fori_loop(0, total // width, one_step, 0)
        for d in range(groups):
            at = slice(d * rows, (d + 1) * rows)
            cos, sin = cos_ref[table_rows(d), :] * scale, sin_ref[table_rows(d), :] * -scale
            outs[d][0, :, cols] = os[at, :]
            outs[d][1, :, cols] = turn(dqs[at, :], cos, sin).astype(BF16)
            outs[d][2, :, cols] = turn(dk[at, :], cos, sin).astype(BF16)
            outs[d][3, :, cols] = dv[at, :].astype(BF16)
        return carry

    lax.fori_loop(0, count, one_head, 0)


SMEM = pl.BlockSpec(memory_space=pltpu.SMEM)
VMEM = pl.BlockSpec(memory_space=pltpu.VMEM)
ANY = pl.BlockSpec(memory_space=pl.ANY)


def body(query_in, key_in, value_in, grad_out, positions, block_flags, band_ids):
    groups = lax.axis_size("seq")
    rows, channels = query_in.shape
    heads = channels // DH // groups
    total = groups * rows
    chunks = math.gcd(CHUNKS, heads)
    count = heads // chunks
    width = 2 * BLK if total % (2 * BLK) == 0 else BLK
    me = lax.axis_index("seq").astype(jnp.int32).reshape(1)
    arrays = (query_in, key_in, value_in, grad_out)
    piece = jax.ShapeDtypeStruct((4, rows, count * DH), BF16)
    pairs = [[(i, i ^ d) for i in range(groups)] for d in range(groups)]
    limit = 40 * 1024 * 1024

    def exchange(pieces):
        return [pieces[0]] + [
            lax.ppermute(pieces[d], "seq", pairs[d]) for d in range(1, groups)
        ]

    def pack(c):
        return pl.pallas_call(
            functools.partial(pack_kernel, groups, heads, c * count, count),
            out_shape=[piece] * groups,
            in_specs=[SMEM] + [ANY] * 4,
            out_specs=[VMEM] * groups,
            scratch_shapes=[pltpu.SemaphoreType.DMA((groups, 4))],
            name=f"pack_{c}",
        )(me, *arrays)

    def attention(pieces, cos, sin):
        area = total * total
        return pl.pallas_call(
            functools.partial(attention_kernel, groups, rows, count, width),
            out_shape=[piece] * groups,
            in_specs=[SMEM] * 3 + [VMEM] * (2 + groups),
            out_specs=[VMEM] * groups,
            scratch_shapes=[pltpu.VMEM((total, DH), BF16)] * 4
            + [pltpu.VMEM((DH, total), BF16)] * 3
            + [pltpu.VMEM((total, width), F32)]
            + [pltpu.VMEM((total, width), BF16)] * 2
            + [pltpu.VMEM((total, DH), F32)] * 2
            + [pltpu.VMEM((total, DH), BF16), pltpu.VMEM((total, DH), F32)],
            compiler_params=pltpu.CompilerParams(vmem_limit_bytes=limit),
            cost_estimate=pl.CostEstimate(
                flops=10 * count * area * DH,
                bytes_accessed=16 * total * count * DH,
                transcendentals=count * area,
            ),
            name="attention",
        )(me, block_flags, band_ids, cos, sin, *pieces)

    def unpack(c, pieces, before):
        kept = len(before)
        return pl.pallas_call(
            functools.partial(unpack_kernel, groups, heads, c * count, count, kept),
            out_shape=[jax.ShapeDtypeStruct((rows, channels), BF16)] * 4,
            in_specs=[SMEM] + [VMEM] * groups + [ANY] * kept,
            out_specs=[ANY] * 4,
            input_output_aliases={1 + groups + a: a for a in range(kept)},
            scratch_shapes=[pltpu.SemaphoreType.DMA((groups, 4))],
            name=f"unpack_{c}",
        )(me, *pieces, *before)

    cos, sin = rope_tables(positions)
    arrived = [exchange(pack(c)) for c in range(chunks)]
    results = ()
    for c in range(chunks):
        results = unpack(c, exchange(attention(arrived[c], cos, sin)), results)
    return tuple(results)


def solution(mesh):
    tokens = P(("clip", "seq"), None)
    return jax.shard_map(
        body,
        mesh=mesh,
        in_specs=(tokens, tokens, tokens, tokens, P(None, "clip"), P("clip", None), P("clip", None)),
        out_specs=(tokens, tokens, tokens, tokens),
        check_vma=False,
    )
```

```python
import functools
import math

import jax
import jax.numpy as jnp
from jax import lax
from jax.experimental import pallas as pl
from jax.experimental.pallas import tpu as pltpu
from jax.sharding import PartitionSpec as P

H = 32
DH = 128
BLK = 128
NTK = 2.0
CHUNKS = 2
LIMIT = 40 * 1024 * 1024

F32 = jnp.float32
BF16 = jnp.bfloat16
NEG_INF = float("-inf")


def rope_tables(positions):
    third = 2 * (DH // 6)
    part_dims = (DH - 2 * third, third, third)
    pieces = []
    for axis_num, dim in enumerate(part_dims):
        base = 10000.0 * NTK ** (dim / (dim - 2.0))
        pair = (jnp.arange(dim, dtype=jnp.int32) // 2).astype(F32)
        inverse = jnp.exp(pair * (-2.0 * math.log(base) / dim))
        pieces.append(positions[axis_num].astype(F32)[:, None] * inverse[None, :])
    angle = jnp.concatenate(pieces, 1)
    sign = jnp.where(jnp.arange(DH, dtype=jnp.int32) % 2 == 0, -1.0, 1.0).astype(F32)
    return jnp.cos(angle), jnp.sin(angle) * sign[None, :]


def pack_kernel(hops, heads, first, count, me_ref, q_ref, k_ref, v_ref, g_ref, *rest):
    groups = len(hops)
    outs, sems = rest[:groups], rest[groups]
    me = me_ref[0]
    copies = []
    for d in range(groups):
        start = pl.multiple_of(((me ^ hops[d]) * heads + first) * DH, DH)
        for a, ref in enumerate((q_ref, k_ref, v_ref, g_ref)):
            copies.append(
                pltpu.make_async_copy(
                    ref.at[:, pl.ds(start, count * DH)], outs[d].at[a], sems.at[d, a]
                )
            )
    for copy in copies:
        copy.start()
    for copy in copies:
        copy.wait()


def unpack_kernel(hops, heads, first, count, kept, me_ref, *rest):
    groups = len(hops)
    pieces = rest[:groups]
    outs = rest[groups + kept : groups + kept + 4]
    sems = rest[groups + kept + 4]
    me = me_ref[0]
    copies = []
    for d in range(groups):
        start = pl.multiple_of(((me ^ hops[d]) * heads + first) * DH, DH)
        for a in range(4):
            copies.append(
                pltpu.make_async_copy(
                    pieces[d].at[a], outs[a].at[:, pl.ds(start, count * DH)], sems.at[d, a]
                )
            )
    for copy in copies:
        copy.start()
    for copy in copies:
        copy.wait()


def dot(x, y):
    return jnp.dot(x, y, preferred_element_type=F32)


def dot_t(x, y):
    return lax.dot_general(x, y, (((1,), (1,)), ((), ())), preferred_element_type=F32)


def attention_kernel(hops, rows, count, width, me_ref, hops_ref, flags_ref, bands_ref, cos_ref, sin_ref, *rest):
    groups = len(hops)
    ins, outs = rest[:groups], rest[groups : 2 * groups]
    qr, kr, vs, gs, kt, vt, gt, scores, low, ds, dk, dv, os, dqs = rest[2 * groups :]
    total = groups * rows
    per_piece = rows // BLK
    blocks = total // BLK
    scale = 1.0 / math.sqrt(DH)
    score_factor = scale / math.log(2.0)
    me = me_ref[0]

    lane = lax.broadcasted_iota(jnp.int32, (DH, DH), 1)
    sublane = lax.broadcasted_iota(jnp.int32, (DH, DH), 0)
    swap = jnp.where((lane ^ 1) == sublane, 1.0, 0.0).astype(BF16)
    even = lax.broadcasted_iota(jnp.int32, (rows, DH), 1) % 2 == 0
    apart = jnp.abs(
        lax.broadcasted_iota(jnp.int32, (BLK, BLK), 0) - lax.broadcasted_iota(jnp.int32, (BLK, BLK), 1)
    )

    def turn_low(x, cos, sin):
        return (x.astype(F32) * cos + dot(x, swap) * sin).astype(BF16)

    def turn(x, cos, sin):
        partner = jnp.where(even, pltpu.roll(x, DH - 1, 1), pltpu.roll(x, 1, 1))
        return (x * cos + partner * sin).astype(BF16)

    def table_rows(d):
        return pl.ds(pl.multiple_of((me ^ hops[d]) * rows, rows), rows)

    def block_of(b):
        return (me ^ hops_ref[b // per_piece]) * per_piece + b % per_piece

    heads = range(count)
    for d in range(groups):
        at = slice(d * rows, (d + 1) * rows)
        cos, sin = cos_ref[table_rows(d), :], sin_ref[table_rows(d), :]
        for h in heads:
            cols = slice(h * DH, (h + 1) * DH)
            qr[h, at, :] = turn_low(ins[d][0, :, cols], cos, sin)
            key = turn_low(ins[d][1, :, cols], cos, sin)
            kr[h, at, :] = key
            kt[h, :, at] = key.T
            value = ins[d][2, :, cols]
            vs[h, at, :] = value
            vt[h, :, at] = value.T
            grad = ins[d][3, :, cols]
            gs[h, at, :] = grad
            gt[h, :, at] = grad.T
    dk[...] = jnp.zeros_like(dk)
    dv[...] = jnp.zeros_like(dv)

    def one_step(i, carry):
        mine = pl.ds(pl.multiple_of(i * width, width), width)
        largest, inverse, delta = {}, {}, {}
        for h in heads:
            query = qr[h, mine, :]
            top = jnp.full((8, width), NEG_INF, F32)
            for j in range(blocks):
                at = slice(j * BLK, (j + 1) * BLK)
                raw = dot_t(kr[h, at, :], query) * score_factor
                parts = []
                for w in range(width // BLK):
                    row, col = block_of(i * (width // BLK) + w), block_of(j)
                    reach = jnp.where(
                        flags_ref[row, col] == 1, jnp.right_shift(BLK, bands_ref[row, col]), 0
                    )
                    parts.append(jnp.where(apart < reach, raw[:, w * BLK : (w + 1) * BLK], NEG_INF))
                part = jnp.concatenate(parts, 1)
                scores[h, at, :] = part
                top = jnp.maximum(top, jnp.max(part.reshape(BLK // 8, 8, width), axis=0))
            largest[h] = jnp.max(top, axis=0, keepdims=True)
        for h in heads:
            norm = jnp.zeros((8, width), F32)
            for j in range(blocks):
                at = slice(j * BLK, (j + 1) * BLK)
                weights = jnp.exp2(scores[h, at, :] - largest[h])
                scores[h, at, :] = weights
                low[h, at, :] = weights.astype(BF16)
                norm = norm + jnp.sum(weights.reshape(BLK // 8, 8, width), axis=0)
            inverse[h] = 1.0 / jnp.sum(norm, axis=0, keepdims=True)
        for h in heads:
            out_t = (dot(vt[h], low[h]) * inverse[h]).astype(BF16).astype(F32)
            grad_t = gt[h, :, mine].astype(F32)
            delta[h] = jnp.sum(out_t * grad_t, axis=0, keepdims=True)
            os[h, mine, :] = out_t.T.astype(BF16)
            dv[h] += dot_t(low[h], (grad_t * inverse[h]).astype(BF16))
        for h in heads:
            grad = gs[h, mine, :]
            for j in range(blocks):
                at = slice(j * BLK, (j + 1) * BLK)
                grad_probs = dot_t(vs[h, at, :], grad)
                ds[h, at, :] = (scores[h, at, :] * ((grad_probs - delta[h]) * inverse[h])).astype(BF16)
        for h in heads:
            dqs[h, mine, :] = dot(kt[h], ds[h]).T
            dk[h] += dot(ds[h], qr[h, mine, :])
        return carry

    lax.fori_loop(0, total // width, one_step, 0, unroll=True)
    for d in range(groups):
        at = slice(d * rows, (d + 1) * rows)
        cos, sin = cos_ref[table_rows(d), :] * scale, sin_ref[table_rows(d), :] * -scale
        for h in heads:
            cols = slice(h * DH, (h + 1) * DH)
            outs[d][0, :, cols] = os[h, at, :]
            outs[d][1, :, cols] = turn(dqs[h, at, :], cos, sin)
            outs[d][2, :, cols] = turn(dk[h, at, :], cos, sin)
            outs[d][3, :, cols] = dv[h, at, :].astype(BF16)


SMEM = pl.BlockSpec(memory_space=pltpu.SMEM)
VMEM = pl.BlockSpec(memory_space=pltpu.VMEM)
ANY = pl.BlockSpec(memory_space=pl.ANY)


def attention_call(hops, count, me, block_flags, band_ids, tables, pieces):
    rows = pieces[0].shape[1]
    total = len(hops) * rows
    width = 2 * BLK if total % (2 * BLK) == 0 else BLK
    area = total * total
    return pl.pallas_call(
        functools.partial(attention_kernel, hops, rows, count, width),
        out_shape=[jax.ShapeDtypeStruct(pieces[0].shape, BF16)] * len(hops),
        in_specs=[SMEM] * 4 + [VMEM] * (len(tables) + len(hops)),
        out_specs=[VMEM] * len(hops),
        scratch_shapes=[pltpu.VMEM((count, total, DH), BF16)] * 4
        + [pltpu.VMEM((count, DH, total), BF16)] * 3
        + [pltpu.VMEM((count, total, width), F32)]
        + [pltpu.VMEM((count, total, width), BF16)] * 2
        + [pltpu.VMEM((count, total, DH), F32)] * 2
        + [pltpu.VMEM((count, total, DH), BF16), pltpu.VMEM((count, total, DH), F32)],
        compiler_params=pltpu.CompilerParams(vmem_limit_bytes=LIMIT),
        cost_estimate=pl.CostEstimate(
            flops=10 * count * area * DH,
            bytes_accessed=16 * total * count * DH,
            transcendentals=count * area,
        ),
        name="attention",
    )(me, jnp.array(hops, jnp.int32), block_flags, band_ids, *tables, *pieces)


def body(query_in, key_in, value_in, grad_out, positions, block_flags, band_ids):
    groups = lax.axis_size("seq")
    rows, channels = query_in.shape
    heads = channels // DH // groups
    chunks = math.gcd(CHUNKS, heads)
    count = heads // chunks
    me = lax.axis_index("seq").astype(jnp.int32).reshape(1)
    arrays = (query_in, key_in, value_in, grad_out)
    piece = jax.ShapeDtypeStruct((4, rows, count * DH), BF16)
    hops = tuple(sorted(range(groups), key=lambda d: (d > 0, -(d >> 1).bit_count(), d & 1, d)))

    def exchange(pieces):
        return [pieces[0]] + [
            lax.ppermute(piece, "seq", [(i, i ^ d) for i in range(groups)])
            for piece, d in zip(pieces[1:], hops[1:])
        ]

    def pack(c):
        return pl.pallas_call(
            functools.partial(pack_kernel, hops, heads, c * count, count),
            out_shape=[piece] * groups,
            in_specs=[SMEM] + [ANY] * 4,
            out_specs=[VMEM] * groups,
            scratch_shapes=[pltpu.SemaphoreType.DMA((groups, 4))],
            name=f"pack_{c}",
        )(me, *arrays)

    def unpack(c, pieces, before):
        kept = len(before)
        return pl.pallas_call(
            functools.partial(unpack_kernel, hops, heads, c * count, count, kept),
            out_shape=[jax.ShapeDtypeStruct((rows, channels), BF16)] * 4,
            in_specs=[SMEM] + [VMEM] * groups + [ANY] * kept,
            out_specs=[ANY] * 4,
            input_output_aliases={1 + groups + a: a for a in range(kept)},
            scratch_shapes=[pltpu.SemaphoreType.DMA((groups, 4))],
            name=f"unpack_{c}",
        )(me, *pieces, *before)

    tables = rope_tables(positions)
    arrived = [exchange(pack(c)) for c in range(chunks)]
    results = ()
    for c in range(chunks):
        turned = exchange(
            attention_call(hops, count, me, block_flags, band_ids, tables, arrived[c])
        )
        results = unpack(c, turned, results)
    return tuple(results)


def solution(mesh):
    tokens = P(("clip", "seq"), None)
    return jax.shard_map(
        body,
        mesh=mesh,
        in_specs=(tokens, tokens, tokens, tokens, P(None, "clip"), P("clip", None), P("clip", None)),
        out_specs=(tokens, tokens, tokens, tokens),
        check_vma=False,
    )
```

```python
import functools
import math

import jax
import jax.numpy as jnp
from jax import lax
from jax.experimental import pallas as pl
from jax.experimental.pallas import tpu as pltpu
from jax.sharding import PartitionSpec as P

H = 32
DH = 128
BLK = 128
NTK = 2.0
CHUNKS = 2
AHEAD = 5
SMALL = 8 * 1024 * 1024
FIRST_CUTS = (0,)
LAST_CUTS = (0,)
LIMIT = 40 * 1024 * 1024

F32 = jnp.float32
BF16 = jnp.bfloat16
NEG_INF = float("-inf")


def rope_tables(positions):
    third = 2 * (DH // 6)
    part_dims = (DH - 2 * third, third, third)
    pieces = []
    for axis_num, dim in enumerate(part_dims):
        base = 10000.0 * NTK ** (dim / (dim - 2.0))
        pair = (jnp.arange(dim, dtype=jnp.int32) // 2).astype(F32)
        inverse = jnp.exp(pair * (-2.0 * math.log(base) / dim))
        pieces.append(positions[axis_num].astype(F32)[:, None] * inverse[None, :])
    angle = jnp.concatenate(pieces, 1)
    sign = jnp.where(jnp.arange(DH, dtype=jnp.int32) % 2 == 0, -1.0, 1.0).astype(F32)
    return jnp.cos(angle), jnp.sin(angle) * sign[None, :]


def pack_kernel(hops, heads, first, count, me_ref, q_ref, k_ref, v_ref, g_ref, *rest):
    groups = len(hops)
    outs, sems = rest[:groups], rest[groups]
    me = me_ref[0]
    copies = []
    for d in range(groups):
        start = pl.multiple_of(((me ^ hops[d]) * heads + first) * DH, DH)
        for a, ref in enumerate((q_ref, k_ref, v_ref, g_ref)):
            copies.append(
                pltpu.make_async_copy(
                    ref.at[:, pl.ds(start, count * DH)], outs[d].at[a], sems.at[d, a]
                )
            )
    for copy in copies:
        copy.start()
    for copy in copies:
        copy.wait()


def unpack_kernel(hops, heads, first, count, kept, me_ref, *rest):
    groups = len(hops)
    pieces = rest[:groups]
    outs = rest[groups + kept : groups + kept + 4]
    sems = rest[groups + kept + 4]
    me = me_ref[0]
    copies = []
    for d in range(groups):
        start = pl.multiple_of(((me ^ hops[d]) * heads + first) * DH, DH)
        for a in range(4):
            copies.append(
                pltpu.make_async_copy(
                    pieces[d].at[a], outs[a].at[:, pl.ds(start, count * DH)], sems.at[d, a]
                )
            )
    for copy in copies:
        copy.start()
    for copy in copies:
        copy.wait()


def dot(x, y):
    return jnp.dot(x, y, preferred_element_type=F32)


def dot_t(x, y):
    return lax.dot_general(x, y, (((1,), (1,)), ((), ())), preferred_element_type=F32)


def attention_kernel(hops, rows, count, width, me_ref, hops_ref, flags_ref, bands_ref, cos_ref, sin_ref, *rest):
    groups = len(hops)
    ins, outs = rest[:groups], rest[groups : 2 * groups]
    qr, kr, vs, gs, kt, vt, gt, scores, low, ds, dk, dv, os, dqs = rest[2 * groups :]
    total = groups * rows
    per_piece = rows // BLK
    blocks = total // BLK
    scale = 1.0 / math.sqrt(DH)
    score_factor = scale / math.log(2.0)
    me = me_ref[0]

    lane = lax.broadcasted_iota(jnp.int32, (DH, DH), 1)
    sublane = lax.broadcasted_iota(jnp.int32, (DH, DH), 0)
    swap = jnp.where((lane ^ 1) == sublane, 1.0, 0.0).astype(BF16)
    even = lax.broadcasted_iota(jnp.int32, (rows, DH), 1) % 2 == 0
    apart = jnp.abs(
        lax.broadcasted_iota(jnp.int32, (BLK, BLK), 0) - lax.broadcasted_iota(jnp.int32, (BLK, BLK), 1)
    )

    def turn_low(x, cos, sin):
        return (x.astype(F32) * cos + dot(x, swap) * sin).astype(BF16)

    def turn(x, cos, sin):
        partner = jnp.where(even, pltpu.roll(x, DH - 1, 1), pltpu.roll(x, 1, 1))
        return (x * cos + partner * sin).astype(BF16)

    def table_rows(d):
        return pl.ds(pl.multiple_of((me ^ hops[d]) * rows, rows), rows)

    def block_of(b):
        return (me ^ hops_ref[b // per_piece]) * per_piece + b % per_piece

    heads = range(count)
    for d in range(groups):
        at = slice(d * rows, (d + 1) * rows)
        cos, sin = cos_ref[table_rows(d), :], sin_ref[table_rows(d), :]
        for h in heads:
            cols = slice(h * DH, (h + 1) * DH)
            qr[h, at, :] = turn_low(ins[d][0, :, cols], cos, sin)
            key = turn_low(ins[d][1, :, cols], cos, sin)
            kr[h, at, :] = key
            kt[h, :, at] = key.T
            value = ins[d][2, :, cols]
            vs[h, at, :] = value
            vt[h, :, at] = value.T
            grad = ins[d][3, :, cols]
            gs[h, at, :] = grad
            gt[h, :, at] = grad.T
    dk[...] = jnp.zeros_like(dk)
    dv[...] = jnp.zeros_like(dv)

    def one_step(i, carry):
        mine = pl.ds(pl.multiple_of(i * width, width), width)
        largest, inverse, delta = {}, {}, {}
        for h in heads:
            query = qr[h, mine, :]
            top = jnp.full((8, width), NEG_INF, F32)
            for j in range(blocks):
                at = slice(j * BLK, (j + 1) * BLK)
                raw = dot_t(kr[h, at, :], query) * score_factor
                parts = []
                for w in range(width // BLK):
                    row, col = block_of(i * (width // BLK) + w), block_of(j)
                    reach = jnp.where(
                        flags_ref[row, col] == 1, jnp.right_shift(BLK, bands_ref[row, col]), 0
                    )
                    parts.append(jnp.where(apart < reach, raw[:, w * BLK : (w + 1) * BLK], NEG_INF))
                part = jnp.concatenate(parts, 1)
                scores[h, at, :] = part
                top = jnp.maximum(top, jnp.max(part.reshape(BLK // 8, 8, width), axis=0))
            largest[h] = jnp.max(top, axis=0, keepdims=True)
        for h in heads:
            norm = jnp.zeros((8, width), F32)
            for j in range(blocks):
                at = slice(j * BLK, (j + 1) * BLK)
                weights = jnp.exp2(scores[h, at, :] - largest[h])
                scores[h, at, :] = weights
                low[h, at, :] = weights.astype(BF16)
                norm = norm + jnp.sum(weights.reshape(BLK // 8, 8, width), axis=0)
            inverse[h] = 1.0 / jnp.sum(norm, axis=0, keepdims=True)
        for h in heads:
            out_t = (dot(vt[h], low[h]) * inverse[h]).astype(BF16).astype(F32)
            grad_t = gt[h, :, mine].astype(F32)
            delta[h] = jnp.sum(out_t * grad_t, axis=0, keepdims=True)
            os[h, mine, :] = out_t.T.astype(BF16)
            dv[h] += dot_t(low[h], (grad_t * inverse[h]).astype(BF16))
        for h in heads:
            grad = gs[h, mine, :]
            for j in range(blocks):
                at = slice(j * BLK, (j + 1) * BLK)
                grad_probs = dot_t(vs[h, at, :], grad)
                ds[h, at, :] = (scores[h, at, :] * ((grad_probs - delta[h]) * inverse[h])).astype(BF16)
        for h in heads:
            dqs[h, mine, :] = dot(kt[h], ds[h]).T
            dk[h] += dot(ds[h], qr[h, mine, :])
        return carry

    lax.fori_loop(0, total // width, one_step, 0, unroll=True)
    for d in range(groups):
        at = slice(d * rows, (d + 1) * rows)
        cos, sin = cos_ref[table_rows(d), :] * scale, sin_ref[table_rows(d), :] * -scale
        for h in heads:
            cols = slice(h * DH, (h + 1) * DH)
            outs[d][0, :, cols] = os[h, at, :]
            outs[d][1, :, cols] = turn(dqs[h, at, :], cos, sin)
            outs[d][2, :, cols] = turn(dk[h, at, :], cos, sin)
            outs[d][3, :, cols] = dv[h, at, :].astype(BF16)


SMEM = pl.BlockSpec(memory_space=pltpu.SMEM)
VMEM = pl.BlockSpec(memory_space=pltpu.VMEM)
ANY = pl.BlockSpec(memory_space=pl.ANY)


def attention_call(hops, count, me, block_flags, band_ids, tables, pieces):
    rows = pieces[0].shape[1]
    total = len(hops) * rows
    width = 2 * BLK if total % (2 * BLK) == 0 else BLK
    area = total * total
    return pl.pallas_call(
        functools.partial(attention_kernel, hops, rows, count, width),
        out_shape=[jax.ShapeDtypeStruct(pieces[0].shape, BF16)] * len(hops),
        in_specs=[SMEM] * 4 + [VMEM] * (len(tables) + len(hops)),
        out_specs=[VMEM] * len(hops),
        scratch_shapes=[pltpu.VMEM((count, total, DH), BF16)] * 4
        + [pltpu.VMEM((count, DH, total), BF16)] * 3
        + [pltpu.VMEM((count, total, width), F32)]
        + [pltpu.VMEM((count, total, width), BF16)] * 2
        + [pltpu.VMEM((count, total, DH), F32)] * 2
        + [pltpu.VMEM((count, total, DH), BF16), pltpu.VMEM((count, total, DH), F32)],
        compiler_params=pltpu.CompilerParams(vmem_limit_bytes=LIMIT),
        cost_estimate=pl.CostEstimate(
            flops=10 * count * area * DH,
            bytes_accessed=16 * total * count * DH,
            transcendentals=count * area,
        ),
        name="attention",
    )(me, jnp.array(hops, jnp.int32), block_flags, band_ids, *tables, *pieces)


def body(query_in, key_in, value_in, grad_out, positions, block_flags, band_ids):
    groups = lax.axis_size("seq")
    rows, channels = query_in.shape
    heads = channels // DH // groups
    chunks = math.gcd(CHUNKS, heads)
    count = heads // chunks
    me = lax.axis_index("seq").astype(jnp.int32).reshape(1)
    arrays = (query_in, key_in, value_in, grad_out)
    piece = jax.ShapeDtypeStruct((4, rows, count * DH), BF16)
    hops = tuple(sorted(range(groups), key=lambda d: (d > 0, -(d >> 1).bit_count(), d & 1, d)))

    def exchange(pieces, start=0):
        return [
            lax.ppermute(piece, "seq", [(i, i ^ d) for i in range(groups)]) if d else piece
            for piece, d in zip(pieces, hops[start:])
        ]

    def pack(c, slots):
        return pl.pallas_call(
            functools.partial(pack_kernel, hops[slots], heads, c * count, count),
            out_shape=[piece] * len(hops[slots]),
            in_specs=[SMEM] + [ANY] * 4,
            out_specs=[VMEM] * len(hops[slots]),
            scratch_shapes=[pltpu.SemaphoreType.DMA((len(hops[slots]), 4))],
            name=f"pack_{c}_{slots.start}",
        )(me, *arrays)

    def unpack(c, slots, pieces, before):
        kept, own = len(before), len(hops[slots])
        return pl.pallas_call(
            functools.partial(unpack_kernel, hops[slots], heads, c * count, count, kept),
            out_shape=[jax.ShapeDtypeStruct((rows, channels), BF16)] * 4,
            in_specs=[SMEM] + [VMEM] * own + [ANY] * kept,
            out_specs=[ANY] * 4,
            input_output_aliases={1 + own + a: a for a in range(kept)},
            scratch_shapes=[pltpu.SemaphoreType.DMA((own, 4))],
            compiler_params=pltpu.CompilerParams(vmem_limit_bytes=SMALL),
            name=f"unpack_{c}_{slots.start}",
        )(me, *pieces[slots], *before)

    def after(pieces, others):
        both = lax.optimization_barrier((*pieces, *others))
        return list(both[: len(pieces)]), list(both[len(pieces) :])

    tables = rope_tables(positions)
    packed = [
        [p for lo, hi in zip(cuts, cuts[1:]) for p in pack(c, slice(lo, hi))]
        for c, cuts in enumerate([FIRST_CUTS + (groups,)] + [(0, groups)] * (chunks - 1))
    ]
    near = AHEAD + 1
    if chunks > 1:
        packed[1], tables = after(packed[1], tables)
    arrived = [exchange(packed[0])]
    turned = []
    for c in range(chunks):
        pending = packed[c + 1] if c + 1 < chunks else turned[-1] if turned else []
        head = exchange(pending[:near])
        new = attention_call(hops, count, me, block_flags, band_ids, tables, arrived[c])
        tail, new = pending[near:], list(new)
        if c + 1 < chunks:
            tail, new = after(tail, new)
        moved = head + exchange(tail, near)
        if c + 1 < chunks:
            arrived.append(moved)
            if c:
                turned[-1] = exchange(turned[-1])
        elif turned:
            turned[-1] = moved
        turned.append(new)
    turned[-1] = exchange(turned[-1])
    results = ()
    for c in range(chunks):
        cuts = LAST_CUTS if c + 1 == chunks else (0,)
        for lo, hi in zip(cuts, cuts[1:] + (groups,)):
            results = unpack(c, slice(lo, hi), turned[c], results)
    return tuple(results)


def solution(mesh):
    tokens = P(("clip", "seq"), None)
    return jax.shard_map(
        body,
        mesh=mesh,
        in_specs=(tokens, tokens, tokens, tokens, P(None, "clip"), P("clip", None), P("clip", None)),
        out_specs=(tokens, tokens, tokens, tokens),
        check_vma=False,
    )
```

```python
import functools
import math

import jax
import jax.numpy as jnp
from jax import lax
from jax.experimental import pallas as pl
from jax.experimental.pallas import tpu as pltpu
from jax.sharding import PartitionSpec as P

H = 32
DH = 128
BLK = 128
NTK = 2.0
CHUNKS = 2
AHEAD = 5
SMALL = 8 * 1024 * 1024
EARLY = 2
LAST = (3,)
LIMIT = 40 * 1024 * 1024

F32 = jnp.float32
BF16 = jnp.bfloat16
NEG_INF = float("-inf")


def rope_tables(positions):
    third = 2 * (DH // 6)
    part_dims = (DH - 2 * third, third, third)
    pieces = []
    for axis_num, dim in enumerate(part_dims):
        base = 10000.0 * NTK ** (dim / (dim - 2.0))
        pair = (jnp.arange(dim, dtype=jnp.int32) // 2).astype(F32)
        inverse = jnp.exp(pair * (-2.0 * math.log(base) / dim))
        pieces.append(positions[axis_num].astype(F32)[:, None] * inverse[None, :])
    angle = jnp.concatenate(pieces, 1)
    sign = jnp.where(jnp.arange(DH, dtype=jnp.int32) % 2 == 0, -1.0, 1.0).astype(F32)
    return jnp.cos(angle), jnp.sin(angle) * sign[None, :]


def pack_kernel(hops, heads, first, count, me_ref, q_ref, k_ref, v_ref, g_ref, *rest):
    groups = len(hops)
    outs, sems = rest[:groups], rest[groups]
    me = me_ref[0]
    copies = []
    for d in range(groups):
        start = pl.multiple_of(((me ^ hops[d]) * heads + first) * DH, DH)
        for a, ref in enumerate((q_ref, k_ref, v_ref, g_ref)):
            copies.append(
                pltpu.make_async_copy(
                    ref.at[:, pl.ds(start, count * DH)], outs[d].at[a], sems.at[d, a]
                )
            )
    for copy in copies:
        copy.start()
    for copy in copies:
        copy.wait()


def unpack_kernel(hops, heads, first, count, kept, me_ref, *rest):
    groups = len(hops)
    pieces = rest[:groups]
    outs = rest[groups + kept : groups + kept + 4]
    sems = rest[groups + kept + 4]
    me = me_ref[0]
    copies = []
    for d in range(groups):
        start = pl.multiple_of(((me ^ hops[d]) * heads + first) * DH, DH)
        for a in range(4):
            copies.append(
                pltpu.make_async_copy(
                    pieces[d].at[a], outs[a].at[:, pl.ds(start, count * DH)], sems.at[d, a]
                )
            )
    for copy in copies:
        copy.start()
    for copy in copies:
        copy.wait()


def dot(x, y):
    return jnp.dot(x, y, preferred_element_type=F32)


def dot_t(x, y):
    return lax.dot_general(x, y, (((1,), (1,)), ((), ())), preferred_element_type=F32)


def attention_kernel(hops, rows, count, width, me_ref, hops_ref, flags_ref, bands_ref, cos_ref, sin_ref, *rest):
    groups = len(hops)
    ins, outs = rest[:groups], rest[groups : 2 * groups]
    qr, kr, vs, gs, kt, vt, gt, scores, low, ds, dk, dv, os, dqs = rest[2 * groups :]
    total = groups * rows
    per_piece = rows // BLK
    blocks = total // BLK
    scale = 1.0 / math.sqrt(DH)
    score_factor = scale / math.log(2.0)
    me = me_ref[0]

    lane = lax.broadcasted_iota(jnp.int32, (DH, DH), 1)
    sublane = lax.broadcasted_iota(jnp.int32, (DH, DH), 0)
    swap = jnp.where((lane ^ 1) == sublane, 1.0, 0.0).astype(BF16)
    even = lax.broadcasted_iota(jnp.int32, (rows, DH), 1) % 2 == 0
    apart = jnp.abs(
        lax.broadcasted_iota(jnp.int32, (BLK, BLK), 0) - lax.broadcasted_iota(jnp.int32, (BLK, BLK), 1)
    )

    def turn_low(x, cos, sin):
        return (x.astype(F32) * cos + dot(x, swap) * sin).astype(BF16)

    def turn(x, cos, sin):
        partner = jnp.where(even, pltpu.roll(x, DH - 1, 1), pltpu.roll(x, 1, 1))
        return (x * cos + partner * sin).astype(BF16)

    def table_rows(d):
        return pl.ds(pl.multiple_of((me ^ hops[d]) * rows, rows), rows)

    def block_of(b):
        return (me ^ hops_ref[b // per_piece]) * per_piece + b % per_piece

    heads = range(count)
    for d in range(groups):
        at = slice(d * rows, (d + 1) * rows)
        cos, sin = cos_ref[table_rows(d), :], sin_ref[table_rows(d), :]
        for h in heads:
            cols = slice(h * DH, (h + 1) * DH)
            qr[h, at, :] = turn_low(ins[d][0, :, cols], cos, sin)
            key = turn_low(ins[d][1, :, cols], cos, sin)
            kr[h, at, :] = key
            kt[h, :, at] = key.T
            value = ins[d][2, :, cols]
            vs[h, at, :] = value
            vt[h, :, at] = value.T
            grad = ins[d][3, :, cols]
            gs[h, at, :] = grad
            gt[h, :, at] = grad.T
    dk[...] = jnp.zeros_like(dk)
    dv[...] = jnp.zeros_like(dv)

    def one_step(i, carry):
        mine = pl.ds(pl.multiple_of(i * width, width), width)
        largest, inverse, delta = {}, {}, {}
        for h in heads:
            query = qr[h, mine, :]
            top = jnp.full((8, width), NEG_INF, F32)
            for j in range(blocks):
                at = slice(j * BLK, (j + 1) * BLK)
                raw = dot_t(kr[h, at, :], query) * score_factor
                parts = []
                for w in range(width // BLK):
                    row, col = block_of(i * (width // BLK) + w), block_of(j)
                    reach = jnp.where(
                        flags_ref[row, col] == 1, jnp.right_shift(BLK, bands_ref[row, col]), 0
                    )
                    parts.append(jnp.where(apart < reach, raw[:, w * BLK : (w + 1) * BLK], NEG_INF))
                part = jnp.concatenate(parts, 1)
                scores[h, at, :] = part
                top = jnp.maximum(top, jnp.max(part.reshape(BLK // 8, 8, width), axis=0))
            largest[h] = jnp.max(top, axis=0, keepdims=True)
        for h in heads:
            norm = jnp.zeros((8, width), F32)
            for j in range(blocks):
                at = slice(j * BLK, (j + 1) * BLK)
                weights = jnp.exp2(scores[h, at, :] - largest[h])
                scores[h, at, :] = weights
                low[h, at, :] = weights.astype(BF16)
                norm = norm + jnp.sum(weights.reshape(BLK // 8, 8, width), axis=0)
            inverse[h] = 1.0 / jnp.sum(norm, axis=0, keepdims=True)
        for h in heads:
            out_t = (dot(vt[h], low[h]) * inverse[h]).astype(BF16).astype(F32)
            grad_t = gt[h, :, mine].astype(F32)
            delta[h] = jnp.sum(out_t * grad_t, axis=0, keepdims=True)
            os[h, mine, :] = out_t.T.astype(BF16)
            dv[h] += dot_t(low[h], (grad_t * inverse[h]).astype(BF16))
        for h in heads:
            grad = gs[h, mine, :]
            for j in range(blocks):
                at = slice(j * BLK, (j + 1) * BLK)
                grad_probs = dot_t(vs[h, at, :], grad)
                ds[h, at, :] = (scores[h, at, :] * ((grad_probs - delta[h]) * inverse[h])).astype(BF16)
        for h in heads:
            dqs[h, mine, :] = dot(kt[h], ds[h]).T
            dk[h] += dot(ds[h], qr[h, mine, :])
        return carry

    lax.fori_loop(0, total // width, one_step, 0, unroll=True)
    for d in range(groups):
        at = slice(d * rows, (d + 1) * rows)
        cos, sin = cos_ref[table_rows(d), :] * scale, sin_ref[table_rows(d), :] * -scale
        for h in heads:
            cols = slice(h * DH, (h + 1) * DH)
            outs[d][0, :, cols] = os[h, at, :]
            outs[d][1, :, cols] = turn(dqs[h, at, :], cos, sin)
            outs[d][2, :, cols] = turn(dk[h, at, :], cos, sin)
            outs[d][3, :, cols] = dv[h, at, :].astype(BF16)


SMEM = pl.BlockSpec(memory_space=pltpu.SMEM)
VMEM = pl.BlockSpec(memory_space=pltpu.VMEM)
ANY = pl.BlockSpec(memory_space=pl.ANY)


def attention_call(hops, count, me, block_flags, band_ids, tables, pieces):
    rows = pieces[0].shape[1]
    total = len(hops) * rows
    width = 2 * BLK if total % (2 * BLK) == 0 else BLK
    area = total * total
    return pl.pallas_call(
        functools.partial(attention_kernel, hops, rows, count, width),
        out_shape=[jax.ShapeDtypeStruct(pieces[0].shape, BF16)] * len(hops),
        in_specs=[SMEM] * 4 + [VMEM] * (len(tables) + len(hops)),
        out_specs=[VMEM] * len(hops),
        scratch_shapes=[pltpu.VMEM((count, total, DH), BF16)] * 4
        + [pltpu.VMEM((count, DH, total), BF16)] * 3
        + [pltpu.VMEM((count, total, width), F32)]
        + [pltpu.VMEM((count, total, width), BF16)] * 2
        + [pltpu.VMEM((count, total, DH), F32)] * 2
        + [pltpu.VMEM((count, total, DH), BF16), pltpu.VMEM((count, total, DH), F32)],
        compiler_params=pltpu.CompilerParams(vmem_limit_bytes=LIMIT),
        cost_estimate=pl.CostEstimate(
            flops=10 * count * area * DH,
            bytes_accessed=16 * total * count * DH,
            transcendentals=count * area,
        ),
        name="attention",
    )(me, jnp.array(hops, jnp.int32), block_flags, band_ids, *tables, *pieces)


def body(query_in, key_in, value_in, grad_out, positions, block_flags, band_ids):
    groups = lax.axis_size("seq")
    rows, channels = query_in.shape
    heads = channels // DH // groups
    chunks = math.gcd(CHUNKS, heads)
    count = heads // chunks
    me = lax.axis_index("seq").astype(jnp.int32).reshape(1)
    arrays = (query_in, key_in, value_in, grad_out)
    piece = jax.ShapeDtypeStruct((4, rows, count * DH), BF16)
    hops = tuple(sorted(range(groups), key=lambda d: (d > 0, -(d >> 1).bit_count(), d & 1, d)))

    def exchange(pieces, start=0):
        return [
            lax.ppermute(piece, "seq", [(i, i ^ d) for i in range(groups)]) if d else piece
            for piece, d in zip(pieces, hops[start:])
        ]

    def pack(c, slots):
        return pl.pallas_call(
            functools.partial(pack_kernel, [hops[s] for s in slots], heads, c * count, count),
            out_shape=[piece] * len(slots),
            in_specs=[SMEM] + [ANY] * 4,
            out_specs=[VMEM] * len(slots),
            scratch_shapes=[pltpu.SemaphoreType.DMA((len(slots), 4))],
            name=f"pack_{c}_{slots[0]}",
        )(me, *arrays)

    def prepare(c):
        order = [*range(1, groups), 0]
        parts = (order[:EARLY], order[EARLY:]) if c == 0 else (order,)
        made = {s: p for slots in parts for s, p in zip(slots, pack(c, slots))}
        return [made[s] for s in range(groups)]

    def unpack(c, slots, pieces, before):
        kept, own = len(before), len(slots)
        return pl.pallas_call(
            functools.partial(unpack_kernel, [hops[s] for s in slots], heads, c * count, count, kept),
            out_shape=[jax.ShapeDtypeStruct((rows, channels), BF16)] * 4,
            in_specs=[SMEM] + [VMEM] * own + [ANY] * kept,
            out_specs=[ANY] * 4,
            input_output_aliases={1 + own + a: a for a in range(kept)},
            scratch_shapes=[pltpu.SemaphoreType.DMA((own, 4))],
            compiler_params=pltpu.CompilerParams(vmem_limit_bytes=SMALL),
            name=f"unpack_{c}_{slots[0]}",
        )(me, *[pieces[s] for s in slots], *before)

    def after(pieces, others):
        both = lax.optimization_barrier((*pieces, *others))
        return list(both[: len(pieces)]), list(both[len(pieces) :])

    near = AHEAD + 1
    tables = rope_tables(positions)
    packed = [prepare(c) for c in range(chunks)]
    if chunks > 1:
        packed[1], tables = after(packed[1], tables)
    arrived = [exchange(packed[0])]
    turned = []
    for c in range(chunks):
        if c + 1 < chunks:
            head = exchange(packed[c + 1][:near])
        new = attention_call(hops, count, me, block_flags, band_ids, tables, arrived[c])
        if c + 1 < chunks:
            tail, new = after(packed[c + 1][near:], new)
            arrived.append(head + exchange(tail, near))
        turned.append(exchange(new))
    results = ()
    for c in range(chunks):
        ends = [*LAST, groups] if c + 1 == chunks else [groups]
        for lo, hi in zip([0] + ends, ends):
            results = unpack(c, range(lo, hi), turned[c], results)
    return tuple(results)


def solution(mesh):
    tokens = P(("clip", "seq"), None)
    return jax.shard_map(
        body,
        mesh=mesh,
        in_specs=(tokens, tokens, tokens, tokens, P(None, "clip"), P("clip", None), P("clip", None)),
        out_specs=(tokens, tokens, tokens, tokens),
        check_vma=False,
    )
```

```python
import functools
import math

import jax
import jax.numpy as jnp
from jax import lax
from jax.experimental import pallas as pl
from jax.experimental.pallas import tpu as pltpu
from jax.sharding import PartitionSpec as P

H = 32
DH = 128
BLK = 128
NTK = 2.0
CHUNKS = 2
AHEAD = 5
SMALL = 8 * 1024 * 1024
EARLY = 2
LAST = (3,)
LIMIT = 40 * 1024 * 1024

F32 = jnp.float32
BF16 = jnp.bfloat16
NEG_INF = float("-inf")


def rope_tables(positions):
    third = 2 * (DH // 6)
    part_dims = (DH - 2 * third, third, third)
    pieces = []
    for axis_num, dim in enumerate(part_dims):
        base = 10000.0 * NTK ** (dim / (dim - 2.0))
        pair = (jnp.arange(dim, dtype=jnp.int32) // 2).astype(F32)
        inverse = jnp.exp(pair * (-2.0 * math.log(base) / dim))
        pieces.append(positions[axis_num].astype(F32)[:, None] * inverse[None, :])
    angle = jnp.concatenate(pieces, 1)
    sign = jnp.where(jnp.arange(DH, dtype=jnp.int32) % 2 == 0, -1.0, 1.0).astype(F32)
    return jnp.cos(angle), jnp.sin(angle) * sign[None, :]


def pack_kernel(hops, heads, first, count, me_ref, q_ref, k_ref, v_ref, g_ref, *rest):
    groups = len(hops)
    outs, sems = rest[:groups], rest[groups]
    me = me_ref[0]
    copies = []
    for d in range(groups):
        start = pl.multiple_of(((me ^ hops[d]) * heads + first) * DH, DH)
        for a, ref in enumerate((q_ref, k_ref, v_ref, g_ref)):
            copies.append(
                pltpu.make_async_copy(
                    ref.at[:, pl.ds(start, count * DH)], outs[d].at[a], sems.at[d, a]
                )
            )
    for copy in copies:
        copy.start()
    for copy in copies:
        copy.wait()


def unpack_kernel(hops, heads, first, count, kept, me_ref, *rest):
    groups = len(hops)
    pieces = rest[:groups]
    outs = rest[groups + kept : groups + kept + 4]
    sems = rest[groups + kept + 4]
    me = me_ref[0]
    copies = []
    for d in range(groups):
        start = pl.multiple_of(((me ^ hops[d]) * heads + first) * DH, DH)
        for a in range(4):
            copies.append(
                pltpu.make_async_copy(
                    pieces[d].at[a], outs[a].at[:, pl.ds(start, count * DH)], sems.at[d, a]
                )
            )
    for copy in copies:
        copy.start()
    for copy in copies:
        copy.wait()


def dot(x, y):
    return jnp.dot(x, y, preferred_element_type=F32)


def dot_t(x, y):
    return lax.dot_general(x, y, (((1,), (1,)), ((), ())), preferred_element_type=F32)


def attention_kernel(hops, rows, count, width, me_ref, hops_ref, flags_ref, bands_ref, cos_ref, sin_ref, *rest):
    groups = len(hops)
    ins, outs = rest[:groups], rest[groups : 2 * groups]
    qr, kr, vs, gs, kt, vt, gt, scores, low, ds, dk, dv, os, dqs = rest[2 * groups :]
    total = groups * rows
    per_piece = rows // BLK
    blocks = total // BLK
    scale = 1.0 / math.sqrt(DH)
    score_factor = scale / math.log(2.0)
    me = me_ref[0]

    lane = lax.broadcasted_iota(jnp.int32, (DH, DH), 1)
    sublane = lax.broadcasted_iota(jnp.int32, (DH, DH), 0)
    swap = jnp.where((lane ^ 1) == sublane, 1.0, 0.0).astype(BF16)
    even = lax.broadcasted_iota(jnp.int32, (rows, DH), 1) % 2 == 0
    apart = jnp.abs(
        lax.broadcasted_iota(jnp.int32, (BLK, BLK), 0) - lax.broadcasted_iota(jnp.int32, (BLK, BLK), 1)
    )

    def turn_low(x, cos, sin):
        return (x.astype(F32) * cos + dot(x, swap) * sin).astype(BF16)

    def turn(x, cos, sin):
        partner = jnp.where(even, pltpu.roll(x, DH - 1, 1), pltpu.roll(x, 1, 1))
        return (x * cos + partner * sin).astype(BF16)

    def table_rows(d):
        return pl.ds(pl.multiple_of((me ^ hops[d]) * rows, rows), rows)

    def block_of(b):
        return (me ^ hops_ref[b // per_piece]) * per_piece + b % per_piece

    heads = range(count)
    for d in range(groups):
        at = slice(d * rows, (d + 1) * rows)
        cos, sin = cos_ref[table_rows(d), :], sin_ref[table_rows(d), :]
        for h in heads:
            cols = slice(h * DH, (h + 1) * DH)
            qr[h, at, :] = turn_low(ins[d][0, :, cols], cos, sin)
            key = turn_low(ins[d][1, :, cols], cos, sin)
            kr[h, at, :] = key
            kt[h, :, at] = key.T
            value = ins[d][2, :, cols]
            vs[h, at, :] = value
            vt[h, :, at] = value.T
            grad = ins[d][3, :, cols]
            gs[h, at, :] = grad
            gt[h, :, at] = grad.T
    dk[...] = jnp.zeros_like(dk)
    dv[...] = jnp.zeros_like(dv)

    def one_step(i, carry):
        mine = pl.ds(pl.multiple_of(i * width, width), width)
        largest, inverse, delta = {}, {}, {}
        for h in heads:
            query = qr[h, mine, :]
            top = jnp.full((8, width), NEG_INF, F32)
            for j in range(blocks):
                at = slice(j * BLK, (j + 1) * BLK)
                raw = dot_t(kr[h, at, :], query) * score_factor
                parts = []
                for w in range(width // BLK):
                    row, col = block_of(i * (width // BLK) + w), block_of(j)
                    reach = jnp.where(
                        flags_ref[row, col] == 1, jnp.right_shift(BLK, bands_ref[row, col]), 0
                    )
                    parts.append(jnp.where(apart < reach, raw[:, w * BLK : (w + 1) * BLK], NEG_INF))
                part = jnp.concatenate(parts, 1)
                scores[h, at, :] = part
                top = jnp.maximum(top, jnp.max(part.reshape(BLK // 8, 8, width), axis=0))
            largest[h] = jnp.max(top, axis=0, keepdims=True)
        for h in heads:
            norm = jnp.zeros((8, width), F32)
            for j in range(blocks):
                at = slice(j * BLK, (j + 1) * BLK)
                weights = jnp.exp2(scores[h, at, :] - largest[h])
                scores[h, at, :] = weights
                low[h, at, :] = weights.astype(BF16)
                norm = norm + jnp.sum(weights.reshape(BLK // 8, 8, width), axis=0)
            inverse[h] = 1.0 / jnp.sum(norm, axis=0, keepdims=True)
        for h in heads:
            out_t = (dot(vt[h], low[h]) * inverse[h]).astype(BF16).astype(F32)
            grad_t = gt[h, :, mine].astype(F32)
            delta[h] = jnp.sum(out_t * grad_t, axis=0, keepdims=True)
            os[h, mine, :] = out_t.T.astype(BF16)
            dv[h] += dot_t(low[h], (grad_t * inverse[h]).astype(BF16))
        for h in heads:
            grad = gs[h, mine, :]
            for j in range(blocks):
                at = slice(j * BLK, (j + 1) * BLK)
                grad_probs = dot_t(vs[h, at, :], grad)
                ds[h, at, :] = (scores[h, at, :] * ((grad_probs - delta[h]) * inverse[h])).astype(BF16)
        for h in heads:
            dqs[h, mine, :] = dot(kt[h], ds[h]).T
            dk[h] += dot(ds[h], qr[h, mine, :])
        return carry

    lax.fori_loop(0, total // width, one_step, 0, unroll=True)
    for d in range(groups):
        at = slice(d * rows, (d + 1) * rows)
        cos, sin = cos_ref[table_rows(d), :] * scale, sin_ref[table_rows(d), :] * -scale
        for h in heads:
            cols = slice(h * DH, (h + 1) * DH)
            outs[d][0, :, cols] = os[h, at, :]
            outs[d][1, :, cols] = turn(dqs[h, at, :], cos, sin)
            outs[d][2, :, cols] = turn(dk[h, at, :], cos, sin)
            outs[d][3, :, cols] = dv[h, at, :].astype(BF16)


SMEM = pl.BlockSpec(memory_space=pltpu.SMEM)
VMEM = pl.BlockSpec(memory_space=pltpu.VMEM)
ANY = pl.BlockSpec(memory_space=pl.ANY)


def attention_call(hops, count, me, block_flags, band_ids, tables, pieces):
    rows = pieces[0].shape[1]
    total = len(hops) * rows
    width = 2 * BLK if total % (2 * BLK) == 0 else BLK
    area = total * total
    return pl.pallas_call(
        functools.partial(attention_kernel, hops, rows, count, width),
        out_shape=[jax.ShapeDtypeStruct(pieces[0].shape, BF16)] * len(hops),
        in_specs=[SMEM] * 4 + [VMEM] * (len(tables) + len(hops)),
        out_specs=[VMEM] * len(hops),
        scratch_shapes=[pltpu.VMEM((count, total, DH), BF16)] * 4
        + [pltpu.VMEM((count, DH, total), BF16)] * 3
        + [pltpu.VMEM((count, total, width), F32)]
        + [pltpu.VMEM((count, total, width), BF16)] * 2
        + [pltpu.VMEM((count, total, DH), F32)] * 2
        + [pltpu.VMEM((count, total, DH), BF16), pltpu.VMEM((count, total, DH), F32)],
        compiler_params=pltpu.CompilerParams(vmem_limit_bytes=LIMIT),
        cost_estimate=pl.CostEstimate(
            flops=10 * count * area * DH,
            bytes_accessed=16 * total * count * DH,
            transcendentals=count * area,
        ),
        name="attention",
    )(me, jnp.array(hops, jnp.int32), block_flags, band_ids, *tables, *pieces)


def body(query_in, key_in, value_in, grad_out, positions, block_flags, band_ids):
    groups = lax.axis_size("seq")
    rows, channels = query_in.shape
    heads = channels // DH // groups
    chunks = math.gcd(CHUNKS, heads)
    count = heads // chunks
    me = lax.axis_index("seq").astype(jnp.int32).reshape(1)
    arrays = (query_in, key_in, value_in, grad_out)
    piece = jax.ShapeDtypeStruct((4, rows, count * DH), BF16)
    hops = tuple(sorted(range(groups), key=lambda d: (d > 0, -(d >> 1).bit_count(), d & 1, d)))

    def exchange(pieces, start=0):
        return [
            lax.ppermute(piece, "seq", [(i, i ^ d) for i in range(groups)]) if d else piece
            for piece, d in zip(pieces, hops[start:])
        ]

    def pack(c, slots):
        return pl.pallas_call(
            functools.partial(pack_kernel, [hops[s] for s in slots], heads, c * count, count),
            out_shape=[pltpu.VMEM(piece.shape, BF16) if c == 0 and len(slots) == EARLY else piece] * len(slots),
            in_specs=[SMEM] + [ANY] * 4,
            out_specs=[VMEM] * len(slots),
            scratch_shapes=[pltpu.SemaphoreType.DMA((len(slots), 4))],
            name=f"pack_{c}_{slots[0]}",
        )(me, *[pltpu.with_memory_space_constraint(a, pltpu.HBM) for a in arrays])

    def prepare(c):
        order = [*range(1, groups), 0]
        parts = (order[:EARLY], order[EARLY:]) if c == 0 else (order,)
        made = {s: p for slots in parts for s, p in zip(slots, pack(c, slots))}
        return [made[s] for s in range(groups)]

    def unpack(c, slots, pieces, before):
        kept, own = len(before), len(slots)
        return pl.pallas_call(
            functools.partial(unpack_kernel, [hops[s] for s in slots], heads, c * count, count, kept),
            out_shape=[jax.ShapeDtypeStruct((rows, channels), BF16)] * 4,
            in_specs=[SMEM] + [VMEM] * own + [ANY] * kept,
            out_specs=[ANY] * 4,
            input_output_aliases={1 + own + a: a for a in range(kept)},
            scratch_shapes=[pltpu.SemaphoreType.DMA((own, 4))],
            compiler_params=pltpu.CompilerParams(vmem_limit_bytes=SMALL),
            name=f"unpack_{c}_{slots[0]}",
        )(me, *[pieces[s] for s in slots], *before)

    def after(pieces, others):
        both = lax.optimization_barrier((*pieces, *others))
        return list(both[: len(pieces)]), list(both[len(pieces) :])

    near = AHEAD + 1
    tables = rope_tables(positions)
    packed = [prepare(c) for c in range(chunks)]
    if chunks > 1:
        packed[1], tables = after(packed[1], tables)
    arrived = [exchange(packed[0])]
    turned = []
    for c in range(chunks):
        if c + 1 < chunks:
            head = exchange(packed[c + 1][:near])
        new = attention_call(hops, count, me, block_flags, band_ids, tables, arrived[c])
        if c + 1 < chunks:
            tail, new = after(packed[c + 1][near:], new)
            arrived.append(head + exchange(tail, near))
        turned.append(exchange(new))
    results = ()
    for c in range(chunks):
        ends = [*LAST, groups] if c + 1 == chunks else [groups]
        for lo, hi in zip([0] + ends, ends):
            results = unpack(c, range(lo, hi), turned[c], results)
    return tuple(results)


def solution(mesh):
    tokens = P(("clip", "seq"), None)
    return jax.shard_map(
        body,
        mesh=mesh,
        in_specs=(tokens, tokens, tokens, tokens, P(None, "clip"), P("clip", None), P("clip", None)),
        out_specs=(tokens, tokens, tokens, tokens),
        check_vma=False,
    )
```

```python
import functools
import math

import jax
import jax.numpy as jnp
from jax import lax
from jax.experimental import pallas as pl
from jax.experimental.pallas import tpu as pltpu
from jax.sharding import PartitionSpec as P

H = 32
DH = 128
BLK = 128
NTK = 2.0
CHUNKS = 2
AHEAD = 5
SMALL = 8 * 1024 * 1024
EARLY = 2
LAST = (3,)
LIMIT = 40 * 1024 * 1024

F32 = jnp.float32
BF16 = jnp.bfloat16
NEG_INF = float("-inf")


def rope_tables(positions):
    third = 2 * (DH // 6)
    part_dims = (DH - 2 * third, third, third)
    pieces = []
    for axis_num, dim in enumerate(part_dims):
        base = 10000.0 * NTK ** (dim / (dim - 2.0))
        pair = (jnp.arange(dim, dtype=jnp.int32) // 2).astype(F32)
        inverse = jnp.exp(pair * (-2.0 * math.log(base) / dim))
        pieces.append(positions[axis_num].astype(F32)[:, None] * inverse[None, :])
    angle = jnp.concatenate(pieces, 1)
    sign = jnp.where(jnp.arange(DH, dtype=jnp.int32) % 2 == 0, -1.0, 1.0).astype(F32)
    return jnp.cos(angle), jnp.sin(angle) * sign[None, :]


def pack_kernel(hops, heads, first, count, me_ref, q_ref, k_ref, v_ref, g_ref, *rest):
    groups = len(hops)
    outs, sems = rest[:groups], rest[groups]
    me = me_ref[0]
    copies = []
    for d in range(groups):
        start = pl.multiple_of(((me ^ hops[d]) * heads + first) * DH, DH)
        for a, ref in enumerate((q_ref, k_ref, v_ref, g_ref)):
            copies.append(
                pltpu.make_async_copy(
                    ref.at[:, pl.ds(start, count * DH)], outs[d].at[a], sems.at[d, a]
                )
            )
    for copy in copies:
        copy.start()
    for copy in copies:
        copy.wait()


def unpack_kernel(hops, heads, first, count, kept, me_ref, *rest):
    groups = len(hops)
    pieces = rest[:groups]
    outs = rest[groups + kept : groups + kept + 4]
    sems = rest[groups + kept + 4]
    me = me_ref[0]
    copies = []
    for d in range(groups):
        start = pl.multiple_of(((me ^ hops[d]) * heads + first) * DH, DH)
        for a in range(4):
            copies.append(
                pltpu.make_async_copy(
                    pieces[d].at[a], outs[a].at[:, pl.ds(start, count * DH)], sems.at[d, a]
                )
            )
    for copy in copies:
        copy.start()
    for copy in copies:
        copy.wait()


def dot(x, y):
    return jnp.dot(x, y, preferred_element_type=F32)


def dot_t(x, y):
    return lax.dot_general(x, y, (((1,), (1,)), ((), ())), preferred_element_type=F32)


def attention_kernel(hops, rows, count, width, me_ref, hops_ref, flags_ref, bands_ref, cos_ref, sin_ref, *rest):
    groups = len(hops)
    ins, outs = rest[:groups], rest[groups : 2 * groups]
    qr, kr, vs, gs, kt, vt, gt, scores, low, ds, dk, dv, os, dqs = rest[2 * groups :]
    total = groups * rows
    per_piece = rows // BLK
    blocks = total // BLK
    scale = 1.0 / math.sqrt(DH)
    score_factor = scale / math.log(2.0)
    me = me_ref[0]

    lane = lax.broadcasted_iota(jnp.int32, (DH, DH), 1)
    sublane = lax.broadcasted_iota(jnp.int32, (DH, DH), 0)
    swap = jnp.where((lane ^ 1) == sublane, 1.0, 0.0).astype(BF16)
    even = lax.broadcasted_iota(jnp.int32, (rows, DH), 1) % 2 == 0
    apart = jnp.abs(
        lax.broadcasted_iota(jnp.int32, (BLK, BLK), 0) - lax.broadcasted_iota(jnp.int32, (BLK, BLK), 1)
    )

    def turn_low(x, cos, sin):
        return (x.astype(F32) * cos + dot(x, swap) * sin).astype(BF16)

    def turn(x, cos, sin):
        partner = jnp.where(even, pltpu.roll(x, DH - 1, 1), pltpu.roll(x, 1, 1))
        return (x * cos + partner * sin).astype(BF16)

    def table_rows(d):
        return pl.ds(pl.multiple_of((me ^ hops[d]) * rows, rows), rows)

    def block_of(b):
        return (me ^ hops_ref[b // per_piece]) * per_piece + b % per_piece

    heads = range(count)
    for d in range(groups):
        at = slice(d * rows, (d + 1) * rows)
        cos, sin = cos_ref[table_rows(d), :], sin_ref[table_rows(d), :]
        for h in heads:
            cols = slice(h * DH, (h + 1) * DH)
            qr[h, at, :] = turn_low(ins[d][0, :, cols], cos, sin)
            key = turn_low(ins[d][1, :, cols], cos, sin)
            kr[h, at, :] = key
            kt[h, :, at] = key.T
            value = ins[d][2, :, cols]
            vs[h, at, :] = value
            vt[h, :, at] = value.T
            grad = ins[d][3, :, cols]
            gs[h, at, :] = grad
            gt[h, :, at] = grad.T
    dk[...] = jnp.zeros_like(dk)
    dv[...] = jnp.zeros_like(dv)

    def one_step(i, carry):
        mine = pl.ds(pl.multiple_of(i * width, width), width)
        largest, inverse, delta = {}, {}, {}
        for h in heads:
            query = qr[h, mine, :]
            top = jnp.full((8, width), NEG_INF, F32)
            for j in range(blocks):
                at = slice(j * BLK, (j + 1) * BLK)
                raw = dot_t(kr[h, at, :], query) * score_factor
                parts = []
                for w in range(width // BLK):
                    row, col = block_of(i * (width // BLK) + w), block_of(j)
                    reach = jnp.where(
                        flags_ref[row, col] == 1, jnp.right_shift(BLK, bands_ref[row, col]), 0
                    )
                    parts.append(jnp.where(apart < reach, raw[:, w * BLK : (w + 1) * BLK], NEG_INF))
                part = jnp.concatenate(parts, 1)
                scores[h, at, :] = part
                top = jnp.maximum(top, jnp.max(part.reshape(BLK // 8, 8, width), axis=0))
            largest[h] = jnp.max(top, axis=0, keepdims=True)
        for h in heads:
            norm = jnp.zeros((8, width), F32)
            for j in range(blocks):
                at = slice(j * BLK, (j + 1) * BLK)
                weights = jnp.exp2(scores[h, at, :] - largest[h])
                scores[h, at, :] = weights
                norm = norm + jnp.sum(weights.reshape(BLK // 8, 8, width), axis=0)
            inverse[h] = 1.0 / jnp.sum(norm, axis=0, keepdims=True)
        for h in heads:
            for j in range(blocks):
                at = slice(j * BLK, (j + 1) * BLK)
                low[h, at, :] = (scores[h, at, :] * inverse[h]).astype(BF16)
        for h in heads:
            out_t = dot(vt[h], low[h]).astype(BF16).astype(F32)
            grad_t = gt[h, :, mine].astype(F32)
            delta[h] = jnp.sum(out_t * grad_t, axis=0, keepdims=True)
            os[h, mine, :] = out_t.T.astype(BF16)
            dv[h] += dot(low[h], gs[h, mine, :])
        for h in heads:
            grad = gs[h, mine, :]
            factor = inverse[h] * scale
            for j in range(blocks):
                at = slice(j * BLK, (j + 1) * BLK)
                grad_probs = dot_t(vs[h, at, :], grad)
                ds[h, at, :] = (scores[h, at, :] * ((grad_probs - delta[h]) * factor)).astype(BF16)
        for h in heads:
            dqs[h, mine, :] = dot(kt[h], ds[h]).T
            dk[h] += dot(ds[h], qr[h, mine, :])
        return carry

    lax.fori_loop(0, total // width, one_step, 0, unroll=True)
    for d in range(groups):
        at = slice(d * rows, (d + 1) * rows)
        cos, sin = cos_ref[table_rows(d), :], -sin_ref[table_rows(d), :]
        for h in heads:
            cols = slice(h * DH, (h + 1) * DH)
            outs[d][0, :, cols] = os[h, at, :]
            outs[d][1, :, cols] = turn(dqs[h, at, :], cos, sin)
            outs[d][2, :, cols] = turn(dk[h, at, :], cos, sin)
            outs[d][3, :, cols] = dv[h, at, :].astype(BF16)


SMEM = pl.BlockSpec(memory_space=pltpu.SMEM)
VMEM = pl.BlockSpec(memory_space=pltpu.VMEM)
ANY = pl.BlockSpec(memory_space=pl.ANY)


def attention_call(hops, count, me, block_flags, band_ids, tables, pieces):
    rows = pieces[0].shape[1]
    total = len(hops) * rows
    width = 2 * BLK if total % (2 * BLK) == 0 else BLK
    area = total * total
    return pl.pallas_call(
        functools.partial(attention_kernel, hops, rows, count, width),
        out_shape=[jax.ShapeDtypeStruct(pieces[0].shape, BF16)] * len(hops),
        in_specs=[SMEM] * 4 + [VMEM] * (len(tables) + len(hops)),
        out_specs=[VMEM] * len(hops),
        scratch_shapes=[pltpu.VMEM((count, total, DH), BF16)] * 4
        + [pltpu.VMEM((count, DH, total), BF16)] * 3
        + [pltpu.VMEM((count, total, width), F32)]
        + [pltpu.VMEM((count, total, width), BF16)] * 2
        + [pltpu.VMEM((count, total, DH), F32)] * 2
        + [pltpu.VMEM((count, total, DH), BF16), pltpu.VMEM((count, total, DH), F32)],
        compiler_params=pltpu.CompilerParams(vmem_limit_bytes=LIMIT),
        cost_estimate=pl.CostEstimate(
            flops=10 * count * area * DH,
            bytes_accessed=16 * total * count * DH,
            transcendentals=count * area,
        ),
        name="attention",
    )(me, jnp.array(hops, jnp.int32), block_flags, band_ids, *tables, *pieces)


def body(query_in, key_in, value_in, grad_out, positions, block_flags, band_ids):
    groups = lax.axis_size("seq")
    rows, channels = query_in.shape
    heads = channels // DH // groups
    chunks = math.gcd(CHUNKS, heads)
    count = heads // chunks
    me = lax.axis_index("seq").astype(jnp.int32).reshape(1)
    arrays = (query_in, key_in, value_in, grad_out)
    piece = jax.ShapeDtypeStruct((4, rows, count * DH), BF16)
    hops = tuple(sorted(range(groups), key=lambda d: (d > 0, -(d >> 1).bit_count(), d & 1, d)))

    def exchange(pieces, start=0):
        return [
            lax.ppermute(piece, "seq", [(i, i ^ d) for i in range(groups)]) if d else piece
            for piece, d in zip(pieces, hops[start:])
        ]

    def pack(c, slots):
        return pl.pallas_call(
            functools.partial(pack_kernel, [hops[s] for s in slots], heads, c * count, count),
            out_shape=[pltpu.VMEM(piece.shape, BF16) if c == 0 and len(slots) == EARLY else piece] * len(slots),
            in_specs=[SMEM] + [ANY] * 4,
            out_specs=[VMEM] * len(slots),
            scratch_shapes=[pltpu.SemaphoreType.DMA((len(slots), 4))],
            name=f"pack_{c}_{slots[0]}",
        )(me, *[pltpu.with_memory_space_constraint(a, pltpu.HBM) for a in arrays])

    def prepare(c):
        order = [*range(1, groups), 0]
        parts = (order[:EARLY], order[EARLY:]) if c == 0 else (order,)
        made = {s: p for slots in parts for s, p in zip(slots, pack(c, slots))}
        return [made[s] for s in range(groups)]

    def unpack(c, slots, pieces, before):
        kept, own = len(before), len(slots)
        return pl.pallas_call(
            functools.partial(unpack_kernel, [hops[s] for s in slots], heads, c * count, count, kept),
            out_shape=[jax.ShapeDtypeStruct((rows, channels), BF16)] * 4,
            in_specs=[SMEM] + [VMEM] * own + [ANY] * kept,
            out_specs=[ANY] * 4,
            input_output_aliases={1 + own + a: a for a in range(kept)},
            scratch_shapes=[pltpu.SemaphoreType.DMA((own, 4))],
            compiler_params=pltpu.CompilerParams(vmem_limit_bytes=SMALL),
            name=f"unpack_{c}_{slots[0]}",
        )(me, *[pieces[s] for s in slots], *before)

    def after(pieces, others):
        both = lax.optimization_barrier((*pieces, *others))
        return list(both[: len(pieces)]), list(both[len(pieces) :])

    near = AHEAD + 1
    tables = rope_tables(positions)
    packed = [prepare(c) for c in range(chunks)]
    if chunks > 1:
        packed[1], tables = after(packed[1], tables)
    arrived = [exchange(packed[0])]
    turned = []
    for c in range(chunks):
        if c + 1 < chunks:
            head = exchange(packed[c + 1][:near])
        new = attention_call(hops, count, me, block_flags, band_ids, tables, arrived[c])
        if c + 1 < chunks:
            tail, new = after(packed[c + 1][near:], new)
            arrived.append(head + exchange(tail, near))
        turned.append(exchange(new))
    results = ()
    for c in range(chunks):
        ends = [*LAST, groups] if c + 1 == chunks else [groups]
        for lo, hi in zip([0] + ends, ends):
            results = unpack(c, range(lo, hi), turned[c], results)
    return tuple(results)


def solution(mesh):
    tokens = P(("clip", "seq"), None)
    return jax.shard_map(
        body,
        mesh=mesh,
        in_specs=(tokens, tokens, tokens, tokens, P(None, "clip"), P("clip", None), P("clip", None)),
        out_specs=(tokens, tokens, tokens, tokens),
        check_vma=False,
    )
```

```python
import functools
import math

import jax
import jax.numpy as jnp
from jax import lax
from jax.experimental import pallas as pl
from jax.experimental.pallas import tpu as pltpu
from jax.sharding import PartitionSpec as P

H = 32
DH = 128
BLK = 128
NTK = 2.0
CHUNKS = 2
AHEAD = 6
SMALL = 8 * 1024 * 1024
EARLY = 2
LAST = (3,)
LIMIT = 40 * 1024 * 1024

F32 = jnp.float32
BF16 = jnp.bfloat16
NEG_INF = float("-inf")


def rope_tables(positions):
    third = 2 * (DH // 6)
    part_dims = (DH - 2 * third, third, third)
    pieces = []
    for axis_num, dim in enumerate(part_dims):
        base = 10000.0 * NTK ** (dim / (dim - 2.0))
        pair = (jnp.arange(dim, dtype=jnp.int32) // 2).astype(F32)
        inverse = jnp.exp(pair * (-2.0 * math.log(base) / dim))
        pieces.append(positions[axis_num].astype(F32)[:, None] * inverse[None, :])
    angle = jnp.concatenate(pieces, 1)
    sign = jnp.where(jnp.arange(DH, dtype=jnp.int32) % 2 == 0, -1.0, 1.0).astype(F32)
    return jnp.cos(angle), jnp.sin(angle) * sign[None, :]


def pack_kernel(hops, heads, first, count, me_ref, q_ref, k_ref, v_ref, g_ref, *rest):
    groups = len(hops)
    outs, sems = rest[:groups], rest[groups]
    me = me_ref[0]
    copies = []
    for d in range(groups):
        start = pl.multiple_of(((me ^ hops[d]) * heads + first) * DH, DH)
        for a, ref in enumerate((q_ref, k_ref, v_ref, g_ref)):
            copies.append(
                pltpu.make_async_copy(
                    ref.at[:, pl.ds(start, count * DH)], outs[d].at[a], sems.at[d, a]
                )
            )
    for copy in copies:
        copy.start()
    for copy in copies:
        copy.wait()


def unpack_kernel(hops, heads, first, count, kept, me_ref, *rest):
    groups = len(hops)
    pieces = rest[:groups]
    outs = rest[groups + kept : groups + kept + 4]
    sems = rest[groups + kept + 4]
    me = me_ref[0]
    copies = []
    for d in range(groups):
        start = pl.multiple_of(((me ^ hops[d]) * heads + first) * DH, DH)
        for a in range(4):
            copies.append(
                pltpu.make_async_copy(
                    pieces[d].at[a], outs[a].at[:, pl.ds(start, count * DH)], sems.at[d, a]
                )
            )
    for copy in copies:
        copy.start()
    for copy in copies:
        copy.wait()


def dot(x, y):
    return jnp.dot(x, y, preferred_element_type=F32)


def dot_t(x, y):
    return lax.dot_general(x, y, (((1,), (1,)), ((), ())), preferred_element_type=F32)


def attention_kernel(hops, rows, count, width, me_ref, hops_ref, flags_ref, bands_ref, cos_ref, sin_ref, *rest):
    groups = len(hops)
    ins, outs = rest[:groups], rest[groups : 2 * groups]
    qr, kr, vs, gs, kt, vt, gt, scores, low, ds, dk, dv, os, dqs = rest[2 * groups :]
    total = groups * rows
    per_piece = rows // BLK
    blocks = total // BLK
    scale = 1.0 / math.sqrt(DH)
    score_factor = scale / math.log(2.0)
    me = me_ref[0]

    lane = lax.broadcasted_iota(jnp.int32, (DH, DH), 1)
    sublane = lax.broadcasted_iota(jnp.int32, (DH, DH), 0)
    swap = jnp.where((lane ^ 1) == sublane, 1.0, 0.0).astype(BF16)
    even = lax.broadcasted_iota(jnp.int32, (rows, DH), 1) % 2 == 0
    apart = jnp.abs(
        lax.broadcasted_iota(jnp.int32, (BLK, BLK), 0) - lax.broadcasted_iota(jnp.int32, (BLK, BLK), 1)
    )

    def turn_low(x, cos, sin):
        return (x.astype(F32) * cos + dot(x, swap) * sin).astype(BF16)

    def turn(x, cos, sin):
        partner = jnp.where(even, pltpu.roll(x, DH - 1, 1), pltpu.roll(x, 1, 1))
        return (x * cos + partner * sin).astype(BF16)

    def table_rows(d):
        return pl.ds(pl.multiple_of((me ^ hops[d]) * rows, rows), rows)

    def block_of(b):
        return (me ^ hops_ref[b // per_piece]) * per_piece + b % per_piece

    heads = range(count)
    for d in range(groups):
        at = slice(d * rows, (d + 1) * rows)
        cos, sin = cos_ref[table_rows(d), :], sin_ref[table_rows(d), :]
        for h in heads:
            cols = slice(h * DH, (h + 1) * DH)
            qr[h, at, :] = turn_low(ins[d][0, :, cols], cos, sin)
            key = turn_low(ins[d][1, :, cols], cos, sin)
            kr[h, at, :] = key
            kt[h, :, at] = key.T
            value = ins[d][2, :, cols]
            vs[h, at, :] = value
            vt[h, :, at] = value.T
            grad = ins[d][3, :, cols]
            gs[h, at, :] = grad
            gt[h, :, at] = grad.T
    dk[...] = jnp.zeros_like(dk)
    dv[...] = jnp.zeros_like(dv)

    def one_step(i, carry):
        mine = pl.ds(pl.multiple_of(i * width, width), width)
        largest, inverse, delta = {}, {}, {}
        for h in heads:
            query = qr[h, mine, :]
            top = jnp.full((8, width), NEG_INF, F32)
            for j in range(blocks):
                at = slice(j * BLK, (j + 1) * BLK)
                raw = dot_t(kr[h, at, :], query) * score_factor
                parts = []
                for w in range(width // BLK):
                    row, col = block_of(i * (width // BLK) + w), block_of(j)
                    reach = jnp.where(
                        flags_ref[row, col] == 1, jnp.right_shift(BLK, bands_ref[row, col]), 0
                    )
                    parts.append(jnp.where(apart < reach, raw[:, w * BLK : (w + 1) * BLK], NEG_INF))
                part = jnp.concatenate(parts, 1)
                scores[h, at, :] = part
                top = jnp.maximum(top, jnp.max(part.reshape(BLK // 8, 8, width), axis=0))
            largest[h] = jnp.max(top, axis=0, keepdims=True)
        for h in heads:
            norm = jnp.zeros((8, width), F32)
            for j in range(blocks):
                at = slice(j * BLK, (j + 1) * BLK)
                weights = jnp.exp2(scores[h, at, :] - largest[h])
                scores[h, at, :] = weights
                norm = norm + jnp.sum(weights.reshape(BLK // 8, 8, width), axis=0)
            inverse[h] = 1.0 / jnp.sum(norm, axis=0, keepdims=True)
        for h in heads:
            for j in range(blocks):
                at = slice(j * BLK, (j + 1) * BLK)
                low[h, at, :] = (scores[h, at, :] * inverse[h]).astype(BF16)
        for h in heads:
            out_t = dot(vt[h], low[h]).astype(BF16).astype(F32)
            grad_t = gt[h, :, mine].astype(F32)
            delta[h] = jnp.sum(out_t * grad_t, axis=0, keepdims=True)
            os[h, mine, :] = out_t.T.astype(BF16)
            dv[h] += dot(low[h], gs[h, mine, :])
        for h in heads:
            grad = gs[h, mine, :]
            factor = inverse[h] * scale
            for j in range(blocks):
                at = slice(j * BLK, (j + 1) * BLK)
                grad_probs = dot_t(vs[h, at, :], grad)
                ds[h, at, :] = (scores[h, at, :] * ((grad_probs - delta[h]) * factor)).astype(BF16)
        for h in heads:
            dqs[h, mine, :] = dot(kt[h], ds[h]).T
            dk[h] += dot(ds[h], qr[h, mine, :])
        return carry

    lax.fori_loop(0, total // width, one_step, 0, unroll=True)
    for d in range(groups):
        at = slice(d * rows, (d + 1) * rows)
        cos, sin = cos_ref[table_rows(d), :], -sin_ref[table_rows(d), :]
        for h in heads:
            cols = slice(h * DH, (h + 1) * DH)
            outs[d][0, :, cols] = os[h, at, :]
            outs[d][1, :, cols] = turn(dqs[h, at, :], cos, sin)
            outs[d][2, :, cols] = turn(dk[h, at, :], cos, sin)
            outs[d][3, :, cols] = dv[h, at, :].astype(BF16)


SMEM = pl.BlockSpec(memory_space=pltpu.SMEM)
VMEM = pl.BlockSpec(memory_space=pltpu.VMEM)
ANY = pl.BlockSpec(memory_space=pl.ANY)


def attention_call(hops, count, me, block_flags, band_ids, tables, pieces):
    rows = pieces[0].shape[1]
    total = len(hops) * rows
    width = 2 * BLK if total % (2 * BLK) == 0 else BLK
    area = total * total
    return pl.pallas_call(
        functools.partial(attention_kernel, hops, rows, count, width),
        out_shape=[jax.ShapeDtypeStruct(pieces[0].shape, BF16)] * len(hops),
        in_specs=[SMEM] * 4 + [VMEM] * (len(tables) + len(hops)),
        out_specs=[VMEM] * len(hops),
        scratch_shapes=[pltpu.VMEM((count, total, DH), BF16)] * 4
        + [pltpu.VMEM((count, DH, total), BF16)] * 3
        + [pltpu.VMEM((count, total, width), F32)]
        + [pltpu.VMEM((count, total, width), BF16)] * 2
        + [pltpu.VMEM((count, total, DH), F32)] * 2
        + [pltpu.VMEM((count, total, DH), BF16), pltpu.VMEM((count, total, DH), F32)],
        compiler_params=pltpu.CompilerParams(vmem_limit_bytes=LIMIT),
        cost_estimate=pl.CostEstimate(
            flops=10 * count * area * DH,
            bytes_accessed=16 * total * count * DH,
            transcendentals=count * area,
        ),
        name="attention",
    )(me, jnp.array(hops, jnp.int32), block_flags, band_ids, *tables, *pieces)


def body(query_in, key_in, value_in, grad_out, positions, block_flags, band_ids):
    groups = lax.axis_size("seq")
    rows, channels = query_in.shape
    heads = channels // DH // groups
    chunks = math.gcd(CHUNKS, heads)
    count = heads // chunks
    me = lax.axis_index("seq").astype(jnp.int32).reshape(1)
    arrays = (query_in, key_in, value_in, grad_out)
    piece = jax.ShapeDtypeStruct((4, rows, count * DH), BF16)
    hops = tuple(sorted(range(groups), key=lambda d: (d > 0, -(d >> 1).bit_count(), d & 1, d)))

    def exchange(pieces, start=0):
        return [
            lax.ppermute(piece, "seq", [(i, i ^ d) for i in range(groups)]) if d else piece
            for piece, d in zip(pieces, hops[start:])
        ]

    def pack(c, slots):
        return pl.pallas_call(
            functools.partial(pack_kernel, [hops[s] for s in slots], heads, c * count, count),
            out_shape=[pltpu.VMEM(piece.shape, BF16) if c == 0 and len(slots) == EARLY else piece] * len(slots),
            in_specs=[SMEM] + [ANY] * 4,
            out_specs=[VMEM] * len(slots),
            scratch_shapes=[pltpu.SemaphoreType.DMA((len(slots), 4))],
            name=f"pack_{c}_{slots[0]}",
        )(me, *[pltpu.with_memory_space_constraint(a, pltpu.HBM) for a in arrays])

    def prepare(c):
        order = [*range(1, groups), 0]
        parts = (order[:EARLY], order[EARLY:]) if c == 0 else (order,)
        made = {s: p for slots in parts for s, p in zip(slots, pack(c, slots))}
        return [made[s] for s in range(groups)]

    def unpack(c, slots, pieces, before):
        kept, own = len(before), len(slots)
        return pl.pallas_call(
            functools.partial(unpack_kernel, [hops[s] for s in slots], heads, c * count, count, kept),
            out_shape=[jax.ShapeDtypeStruct((rows, channels), BF16)] * 4,
            in_specs=[SMEM] + [VMEM] * own + [ANY] * kept,
            out_specs=[ANY] * 4,
            input_output_aliases={1 + own + a: a for a in range(kept)},
            scratch_shapes=[pltpu.SemaphoreType.DMA((own, 4))],
            compiler_params=pltpu.CompilerParams(vmem_limit_bytes=SMALL),
            name=f"unpack_{c}_{slots[0]}",
        )(me, *[pieces[s] for s in slots], *before)

    def after(pieces, others):
        both = lax.optimization_barrier((*pieces, *others))
        return list(both[: len(pieces)]), list(both[len(pieces) :])

    near = AHEAD + 1
    tables = rope_tables(positions)
    packed = [prepare(c) for c in range(chunks)]
    if chunks > 1:
        packed[1], tables = after(packed[1], tables)
    arrived = [exchange(packed[0])]
    turned = []
    for c in range(chunks):
        if c + 1 < chunks:
            head = exchange(packed[c + 1][:near])
        new = attention_call(hops, count, me, block_flags, band_ids, tables, arrived[c])
        if c + 1 < chunks:
            tail, new = after(packed[c + 1][near:], new)
            arrived.append(head + exchange(tail, near))
        turned.append(exchange(new))
    results = ()
    for c in range(chunks):
        ends = [*LAST, groups] if c + 1 == chunks else [groups]
        for lo, hi in zip([0] + ends, ends):
            results = unpack(c, range(lo, hi), turned[c], results)
    return tuple(results)


def solution(mesh):
    tokens = P(("clip", "seq"), None)
    return jax.shard_map(
        body,
        mesh=mesh,
        in_specs=(tokens, tokens, tokens, tokens, P(None, "clip"), P("clip", None), P("clip", None)),
        out_specs=(tokens, tokens, tokens, tokens),
        check_vma=False,
    )
```
